32 devices in a mesh: shots: 2 (over y), depth: 4 (over x, core), strip: 4 (over z).
Axes of the slice: x: 2, y: 2, z: 4, core: 2. Of those that a mesh axis runs over, the one named last changes fastest.
Arguments:
- surface: float32 [2, 8, 32, 2048], P(None, 'shots', 'strip'), parts along dimension 1, may hold values from -6 to 6
- omegas: float32 [4], replicated, may hold values from 1 to 3
- region_speed: float32 [8], replicated, may hold values from 1 to 2
- fd_coeff: float32 [8], replicated, may hold values from 0.02 to 0.08
- region_index: int32 [12, 32, 2048], P('depth', 'strip'), may hold values from 0 to 7
- ref_region: int32 [12], P('depth'), may hold values from 0 to 7
Outputs:
- image: float32 [12, 32, 4096], P('depth', 'strip', 'shots'), parts along dimension 2
The draws below stay inside these ranges and needn't reach their ends.
There are 2 independent parts, one for each index of `shots`. The reference program is written for one: setup_inputs(seed, part) draws one part's arguments, and reference() takes and returns one part's arrays. A program takes and returns all parts, laid end to end along the dimension named above; an argument that names none is the same for every part. Nothing has to cross between parts.
All inputs are finite; a program needn't handle non-finite values.
Results may differ from the reference program's by a relative error of at most 0.00015.
Values sent between devices are 32-bit elements; how exact they have to be, the bound alone decides.
A program may use at most 64 MiB of HBM per device.

```python
import math
import jax
import jax.numpy as jnp
from jax import lax

NX = 2048
FREQ = 4
REGIONS = 8
NY = 32
DEPTHS = 12


def set_ends(values, rng, smallest, high):
    place = [jax.random.randint(jax.random.fold_in(rng, axis), (), 0, length) for axis, length in enumerate(values.shape)]
    longest = values.shape.index(max(values.shape))
    beside = place[:longest] + [(place[longest] + 1) % values.shape[longest]] + place[longest + 1:]
    return values.at[tuple(place)].set(smallest).at[tuple(beside)].set(high)


def block_levels(stream_key, dims, pieces, smallest, top_value):
    def one(dim, shards_of):
        steps = jax.random.uniform(jax.random.fold_in(jax.random.fold_in(stream_key, 6), dim), (shards_of,), jnp.float32, smallest / len(pieces), top_value / len(pieces))
        return jnp.repeat(jnp.exp(steps), dims[dim] // shards_of).reshape((-1,) + (1,) * (len(dims) - dim - 1))

    loudness = one(*pieces[0])
    for cut in pieces[1:]:
        loudness = loudness * one(*cut)
    return loudness


def centred(rng, dims, width, bound, split=(), kind=jnp.bfloat16):
    drawn = width * jax.random.normal(rng, dims, jnp.float32)
    if split:
        drawn = drawn * block_levels(rng, dims, split, -0.22, 0.18)
    return jnp.clip(drawn, -bound, bound).astype(kind)


def setup_inputs(seed: int = 0, part: int = 0) -> dict:
    arg_keys = jax.random.split(jax.random.key(seed), 7)
    own_keys = jax.random.split(jax.random.fold_in(arg_keys[6], part), 7)
    return {
        "surface": centred(own_keys[0], (2, FREQ, NY, NX), 1.0, 6.0, ((2, 4),), jnp.float32),
        "omegas": jnp.clip(jnp.exp(jax.random.uniform(arg_keys[1], (FREQ,), jnp.float32, math.log(1.0), math.log(3.0))), 1.0, 3.0),
        "region_speed": jnp.clip(jax.random.uniform(arg_keys[2], (REGIONS,), jnp.float32, 1.0, 2.0), 1.0, 2.0),
        "fd_coeff": jnp.clip(jnp.exp(jax.random.uniform(arg_keys[3], (REGIONS,), jnp.float32, math.log(0.02), math.log(0.08))), 0.02, 0.08),
        "region_index": set_ends(jax.random.randint(arg_keys[4], (DEPTHS, NY, NX), 0, REGIONS), jax.random.fold_in(arg_keys[4], 1), 0, REGIONS - 1).astype(jnp.int32),
        "ref_region": set_ends(jax.random.randint(arg_keys[5], (DEPTHS,), 0, REGIONS), jax.random.fold_in(arg_keys[5], 1), 0, REGIONS - 1).astype(jnp.int32),
    }


DAMPING = 0.05

def wave_numbers():
    counter = jnp.arange(NX)
    signed = jnp.where(counter >= NX // 2, counter - NX, counter)
    return signed.astype(jnp.float32) * (2.0 * math.pi / NX)

def laplace_rows(values):
    padded = jnp.pad(values, ((1, 1), (0, 0)))
    return padded[:-2] + padded[2:] + jnp.roll(values, 1, 1) + jnp.roll(values, -1, 1) - 4.0 * values

def advance(real_part, imag_part, omega_now, slow_cells, coef_cells, ref_slow, kx_line):
    wave_ref = omega_now * ref_slow
    excess = wave_ref * wave_ref - kx_line * kx_line
    decay_line = jnp.exp(-jnp.sqrt(jnp.maximum(-excess, 0.0)))
    vertical = jnp.sqrt(jnp.maximum(excess, 0.0))
    spectrum = jnp.fft.fft(lax.complex(real_part, imag_part), axis=-1)
    spectrum = spectrum * lax.complex(decay_line * jnp.cos(vertical), decay_line * jnp.sin(vertical))
    shifted = jnp.fft.ifft(spectrum, axis=-1)
    shift_re = jnp.real(shifted)
    shift_im = jnp.imag(shifted)
    phase_cell = omega_now * (slow_cells - ref_slow)
    cosine = jnp.cos(phase_cell)
    sine_part = jnp.sin(phase_cell)
    turned_re = shift_re * cosine - shift_im * sine_part
    turned_im = shift_re * sine_part + shift_im * cosine
    lap_re = laplace_rows(turned_re)
    lap_im = laplace_rows(turned_im)
    stencil_gain = coef_cells / omega_now
    new_re = turned_re + (lap_re * DAMPING - lap_im * stencil_gain)
    new_im = turned_im + (lap_re * stencil_gain + lap_im * DAMPING)
    return (new_re, new_im)

def reference(surface, omegas, region_speed, fd_coeff, region_index, ref_region):
    inv_speed = 1.0 / region_speed
    slowness = inv_speed[region_index]
    coefficient = fd_coeff[region_index]
    ref_slowness = inv_speed[ref_region]
    kx_line = wave_numbers()
    layers = [jnp.zeros((NY, NX), jnp.float32) for depth_no in range(DEPTHS)]
    for freq_no in range(FREQ):
        omega_now = omegas[freq_no]
        real_part = surface[0, freq_no]
        imag_part = surface[1, freq_no]
        for depth_no in range(DEPTHS):
            real_part, imag_part = advance(real_part, imag_part, omega_now, slowness[depth_no], coefficient[depth_no], ref_slowness[depth_no], kx_line)
            layers[depth_no] = layers[depth_no] + real_part
    return jnp.stack(layers)
```

```python
import functools
import math

import jax
import jax.numpy as jnp
import ml_dtypes
import numpy as np
from jax import lax
from jax.experimental import pallas as pl
from jax.experimental.pallas import tpu as pltpu
from jax.sharding import PartitionSpec as P

DAMPING = 0.05
LANES = 128
RADIX = 16
LEAD = 3
SQUARE_MAX = 9.5
MESH = pl.DeviceIdType.MESH


def fitted(function, terms):
    nodes = 0.5 * SQUARE_MAX * (1.0 - np.cos((np.arange(64) + 0.5) * np.pi / 64))
    fit = np.polynomial.Chebyshev.fit(nodes, function(np.sqrt(nodes)), terms - 1, domain=[0, SQUARE_MAX])
    return [float(c) for c in fit.convert(kind=np.polynomial.Polynomial).coef]


COS_TERMS = fitted(np.cos, 9)
SINC_TERMS = fitted(lambda x: np.sin(x) / x, 9)


def horner(terms, square):
    value = jnp.full(square.shape, terms[-1], jnp.float32)
    for term in reversed(terms[:-1]):
        value = value * square + term
    return value


def tables(line_len):
    inner = np.arange(LANES)
    outer = np.arange(RADIX)
    angle = 2.0 * np.pi * (inner[:, None] * inner[None, :] % LANES) / LANES
    cosine, sine = np.cos(angle), np.sin(angle)
    matrix = np.block([[cosine, -sine], [sine, cosine]])
    high = matrix.astype(ml_dtypes.bfloat16)
    low = (matrix - high.astype(np.float64)).astype(ml_dtypes.bfloat16)
    weights = np.concatenate([high, high, low])
    twist = 2.0 * np.pi * (outer[:, None] * inner[None, :]) / line_len
    twiddle = np.stack([np.cos(twist), np.sin(twist)]).astype(np.float32)
    wave = outer[:, None] + RADIX * inner[None, :]
    signed = np.where(wave >= line_len // 2, wave - line_len, wave)
    kx = signed.astype(np.float32) * np.float32(2.0 * math.pi / line_len)
    return weights, twiddle, kx


def add(a, b):
    return a[0] + b[0], a[1] + b[1]


def sub(a, b):
    return a[0] - b[0], a[1] - b[1]


def times(a, c, s):
    return a[0] * c - a[1] * s, a[0] * s + a[1] * c


def dft4(z):
    even, odd = add(z[0], z[2]), add(z[1], z[3])
    p, r = sub(z[0], z[2]), sub(z[1], z[3])
    turned = (r[1], -r[0])
    return [add(even, odd), (p[0] + r[1], p[1] - r[0]), sub(even, odd), (p[0] - r[1], p[1] + r[0])]


def twist16(z, power):
    if power == 0:
        return z
    if power == 4:
        return z[1], -z[0]
    h = math.sqrt(0.5)
    if power == 2:
        return (z[0] + z[1]) * h, (z[1] - z[0]) * h
    if power == 6:
        return (z[1] - z[0]) * h, (z[0] + z[1]) * (-h)
    angle = -2.0 * math.pi * power / 16
    return times(z, math.cos(angle), math.sin(angle))


def dft16(z):
    mid = [[twist16(v, n * k) for k, v in enumerate(dft4([z[4 * m + n] for m in range(4)]))] for n in range(4)]
    out = [None] * 16
    for k in range(4):
        for j, v in enumerate(dft4([mid[n][k] for n in range(4)])):
            out[k + 4 * j] = v
    return out


def dft128(z, weights):
    stacked = jnp.concatenate(
        [jnp.concatenate([v[0] for v in z], 0), jnp.concatenate([v[1] for v in z], 0)], 1
    )
    high = stacked.astype(jnp.bfloat16)
    low = (stacked - high.astype(jnp.float32)).astype(jnp.bfloat16)
    wide = jnp.concatenate([high, low, high], 1)
    out = jnp.dot(wide, weights, preferred_element_type=jnp.float32)
    rows = z[0][0].shape[0]
    return [
        (out[c * rows:(c + 1) * rows, :LANES], out[c * rows:(c + 1) * rows, LANES:])
        for c in range(len(z))
    ]


def kernel(
    sections, strips, surface, omegas, speeds, coeffs, region, refs, weights, twiddle, kx,
    image,
    wave, regions, ref_slow, ref_send, halo_out, halo_in, parts_out, parts_in, mult, phase, gain, gain_rows, partial,
    in_sem, ref_ssem, ref_rsem, reg_ssem, reg_rsem, halo_ssem, halo_rsem, img_ssem, img_rsem,
):
    me = lax.axis_index("depth")
    strip = lax.axis_index("strip")
    per = region.shape[0]
    steps = per * sections
    rows = region.shape[1]
    line_len = region.shape[2]
    chunks = line_len // LANES
    tile = (rows, LANES)
    region_count = speeds.shape[0]

    load = pltpu.make_async_copy(surface.at[:, me], wave, in_sem)
    load.start()

    barrier = pltpu.get_barrier_semaphore()
    for delta in range(1, sections):
        pl.semaphore_signal(barrier, 1, device_id={"depth": lax.rem(me + delta, sections)}, device_id_type=MESH)

    @pl.when(strip > 0)
    def _():
        pl.semaphore_signal(barrier, 1, device_id={"strip": strip - 1}, device_id_type=MESH)

    @pl.when(strip < strips - 1)
    def _():
        pl.semaphore_signal(barrier, 1, device_id={"strip": strip + 1}, device_id_type=MESH)

    row_no = lax.broadcasted_iota(jnp.int32, tile, 0)
    lane_no = lax.broadcasted_iota(jnp.int32, tile, 1)
    omega = jnp.zeros(tile, jnp.float32)
    for f in range(sections):
        omega = jnp.where(jnp.full(tile, me, jnp.int32) == f, omegas[f], omega)
    speed_rows = jnp.full(tile, 1.0, jnp.float32)
    coeff_rows = jnp.zeros(tile, jnp.float32)
    for r in range(region_count):
        speed_rows = jnp.where(row_no == r, speeds[r], speed_rows)
        coeff_rows = jnp.where(row_no == r, coeffs[r], coeff_rows)
    inv_rows = 1.0 / speed_rows
    gain_rows[...] = coeff_rows / omega
    for j in range(per):
        chosen = jnp.full(tile, refs[j], jnp.int32)
        speed_here = jnp.full(tile, 1.0, jnp.float32)
        for r in range(region_count):
            speed_here = jnp.where(chosen == r, speeds[r], speed_here)
        ref_send[j] = 1.0 / speed_here
        ref_slow[me * per + j] = 1.0 / speed_here
        regions[me * per + j] = region[j]

    @pl.when(strip == 0)
    def _():
        halo_in[0] = jnp.zeros(halo_in.shape[1:], jnp.float32)

    @pl.when(strip == strips - 1)
    def _():
        halo_in[1] = jnp.zeros(halo_in.shape[1:], jnp.float32)

    def ref_copy(delta):
        return pltpu.make_async_remote_copy(
            ref_send, ref_slow.at[pl.ds(me * per, per)], ref_ssem.at[delta], ref_rsem.at[me],
            device_id={"depth": lax.rem(me + delta, sections)}, device_id_type=MESH,
        )

    def region_copy(j, delta):
        return pltpu.make_async_remote_copy(
            region.at[j], regions.at[me * per + j], reg_ssem.at[delta, j], reg_rsem.at[me * per + j],
            device_id={"depth": lax.rem(me + delta, sections)}, device_id_type=MESH,
        )

    def halo_copy(k, side):
        return pltpu.make_async_remote_copy(
            halo_out.at[side, k], halo_in.at[side, k], halo_ssem.at[side, k], halo_rsem.at[side, k],
            device_id={"strip": strip + 1 - 2 * side}, device_id_type=MESH,
        )

    def image_copy(k):
        return pltpu.make_async_remote_copy(
            parts_out.at[k], parts_in.at[me, lax.rem(k, per)], img_ssem.at[k], img_rsem.at[me, lax.rem(k, per)],
            device_id={"depth": k // per}, device_id_type=MESH,
        )

    pl.semaphore_wait(barrier, sections - 1 + jnp.minimum(strip, 1) + jnp.minimum(strips - 1 - strip, 1))

    for delta in range(1, sections):
        ref_copy(delta).start()

    def send_region(k):
        @pl.when(k // per == me)
        def _():
            for delta in range(1, sections):
                region_copy(lax.rem(k, per), delta).start()

    for k in range(LEAD):
        send_region(jnp.int32(k))
    load.wait()
    for delta in range(1, sections):
        source = lax.rem(me + delta, sections)
        pltpu.make_async_remote_copy(
            ref_send, ref_slow.at[pl.ds(source * per, per)], ref_ssem.at[delta], ref_rsem.at[source],
            device_id={"depth": source}, device_id_type=MESH,
        ).wait_recv()

    def prepare(k, slot):
        ref = ref_slow[k]
        wave_ref = omega[:1] * ref[:1]
        excess = wave_ref * wave_ref - kx[...] * kx[...]
        root = jnp.sqrt(jnp.abs(excess))
        live = excess >= 0.0
        square = jnp.maximum(excess, 0.0)
        scale = 1.0 / line_len
        mult[0] = jnp.where(live, horner(COS_TERMS, square), jnp.exp(-root)) * scale
        mult[1] = jnp.where(live, root * horner(SINC_TERMS, square), 0.0) * scale
        angle = omega * (inv_rows - ref)
        square = angle * angle
        turn_cos = horner(COS_TERMS, square)
        turn_sin = angle * horner(SINC_TERMS, square)

        @pl.when(k // per != me)
        def _():
            pltpu.make_async_remote_copy(
                region.at[0], regions.at[k], reg_ssem.at[0, 0], reg_rsem.at[k],
                device_id={"depth": me}, device_id_type=MESH,
            ).wait_recv()

        gains = gain_rows[...]
        spread = [
            [jnp.broadcast_to(t[r:r + 1], tile) for r in range(region_count)] for t in (turn_cos, turn_sin, gains)
        ]
        for a in range(chunks):
            cols = slice(a * LANES, (a + 1) * LANES)
            cells = regions[k, :, cols]
            masks = [(cells & bit) != 0 for bit in (1, 2, 4)]
            found = []
            for level in spread:
                for mask in masks:
                    level = [jnp.where(mask, level[2 * i + 1], level[2 * i]) for i in range(len(level) // 2)]
                found.append(level[0])
            phase[0, :, cols] = found[0]
            phase[1, :, cols] = found[1]
            gain[slot, :, cols] = found[2]

    prepare(jnp.int32(0), 0)

    def step(k, carry):
        slot = lax.rem(k, 2)

        @pl.when(k + LEAD < steps)
        def _():
            send_region(k + LEAD)

        def chunk(ref, *lead):
            return [ref[(*lead, slice(None), slice(a * LANES, (a + 1) * LANES))] for a in range(chunks)]

        z = list(zip(chunk(wave, 0), chunk(wave, 1)))
        z = dft16(z)
        twist = [(twiddle[0, c:c + 1], -twiddle[1, c:c + 1]) for c in range(chunks)]
        z = [z[0]] + [times(z[c], *twist[c]) for c in range(1, chunks)]
        z = dft128(z, weights[...])
        z = [times(z[c], mult[0, c:c + 1], mult[1, c:c + 1]) for c in range(chunks)]
        z = [(v[1], v[0]) for v in z]
        z = dft128(z, weights[...])
        z = [z[0]] + [times(z[c], *twist[c]) for c in range(1, chunks)]
        z = dft16(z)
        z = [(v[1], v[0]) for v in z]
        v = [times(z[a], pc, ps) for a, (pc, ps) in enumerate(zip(chunk(phase, 0), chunk(phase, 1)))]
        for a in range(chunks):
            for part in range(2):
                halo_out[0, k, part * chunks + a:part * chunks + a + 1] = v[a][part][rows - 1:]
                halo_out[1, k, part * chunks + a:part * chunks + a + 1] = v[a][part][:1]

        @pl.when(strip < strips - 1)
        def _():
            halo_copy(k, 0).start()

        @pl.when(strip > 0)
        def _():
            halo_copy(k, 1).start()

        lap = []
        for part in range(2):
            right = [pltpu.roll(v[a][part], 1, 1) for a in range(chunks)]
            left = [pltpu.roll(v[a][part], LANES - 1, 1) for a in range(chunks)]
            sums = []
            for a in range(chunks):
                here = v[a][part]
                before = jnp.where(lane_no == 0, right[a - 1], right[a])
                after = jnp.where(lane_no == LANES - 1, left[(a + 1) % chunks], left[a])
                above = jnp.where(row_no == 0, 0.0, pltpu.roll(here, 1, 0))
                below = jnp.where(row_no == rows - 1, 0.0, pltpu.roll(here, rows - 1, 0))
                sums.append(above + below + before + after - 4.0 * here)
            lap.append(sums)
        gains = chunk(gain, slot)
        for a in range(chunks):
            cols = slice(a * LANES, (a + 1) * LANES)
            lr, li = lap[0][a], lap[1][a]
            partial[0, :, cols] = v[a][0] + (DAMPING * lr - gains[a] * li)
            partial[1, :, cols] = v[a][1] + (gains[a] * lr + DAMPING * li)

        @pl.when(k + 1 < steps)
        def _():
            prepare(k + 1, 1 - slot)

        @pl.when(strip > 0)
        def _():
            halo_copy(k, 0).wait_recv()

        @pl.when(strip < strips - 1)
        def _():
            halo_copy(k, 1).wait_recv()

        gains = chunk(gain, slot)
        for a in range(chunks):
            cols = slice(a * LANES, (a + 1) * LANES)
            edge = []
            for part in range(2):
                at = part * chunks + a
                top = jnp.broadcast_to(halo_in[0, k, at:at + 1], tile)
                low = jnp.broadcast_to(halo_in[1, k, at:at + 1], tile)
                edge.append(jnp.where(row_no == 0, top, jnp.where(row_no == rows - 1, low, 0.0)))
            er, ei = edge
            new_re = partial[0, :, cols] + (DAMPING * er - gains[a] * ei)
            wave[0, :, cols] = new_re
            wave[1, :, cols] = partial[1, :, cols] + (gains[a] * er + DAMPING * ei)
            parts_out[k, :, cols] = new_re

        @pl.when(k // per != me)
        def _():
            image_copy(k).start()

        return carry

    lax.fori_loop(0, steps, step, 0)

    for j in range(per):
        for delta in range(1, sections):
            source = lax.rem(me + delta, sections)
            pltpu.make_async_remote_copy(
                parts_out.at[0], parts_in.at[source, j], img_ssem.at[0], img_rsem.at[source, j],
                device_id={"depth": source}, device_id_type=MESH,
            ).wait_recv()
        total = parts_out[me * per + j]
        for delta in range(1, sections):
            total = total + parts_in[lax.rem(me + delta, sections), j]
        image[j] = total

    for delta in range(1, sections):
        ref_copy(delta).wait_send()
        for j in range(per):
            region_copy(j, delta).wait_send()

    def drain(k, carry):
        @pl.when(k // per != me)
        def _():
            image_copy(k).wait_send()

        @pl.when(strip < strips - 1)
        def _():
            halo_copy(k, 0).wait_send()

        @pl.when(strip > 0)
        def _():
            halo_copy(k, 1).wait_send()

        return carry

    lax.fori_loop(0, steps, drain, 0)


def shards(sections, strips, surface, omegas, region_speed, fd_coeff, region_index, ref_region):
    freq_count, rows, line_len = surface.shape[1:]
    per = region_index.shape[0]
    steps = per * sections
    chunks = line_len // LANES
    assert freq_count == sections and chunks == RADIX
    weights, twiddle, kx = tables(line_len)
    f32 = jnp.float32
    vmem = pl.BlockSpec(memory_space=pltpu.VMEM)
    smem = pl.BlockSpec(memory_space=pltpu.SMEM)
    dma = pltpu.SemaphoreType.DMA
    return pl.pallas_call(
        functools.partial(kernel, sections, strips),
        out_shape=jax.ShapeDtypeStruct((per, rows, line_len), f32),
        in_specs=[pl.BlockSpec(memory_space=pl.ANY), smem, smem, smem, vmem, smem, vmem, vmem, vmem],
        out_specs=vmem,
        scratch_shapes=[
            pltpu.VMEM((2, rows, line_len), f32),
            pltpu.VMEM((steps, rows, line_len), jnp.int32),
            pltpu.VMEM((steps, rows, LANES), f32),
            pltpu.VMEM((per, rows, LANES), f32),
            pltpu.VMEM((2, steps, 2 * chunks, LANES), f32),
            pltpu.VMEM((2, steps, 2 * chunks, LANES), f32),
            pltpu.VMEM((steps, rows, line_len), f32),
            pltpu.VMEM((sections, per, rows, line_len), f32),
            pltpu.VMEM((2, chunks, LANES), f32),
            pltpu.VMEM((2, rows, line_len), f32),
            pltpu.VMEM((2, rows, line_len), f32),
            pltpu.VMEM((rows, LANES), f32),
            pltpu.VMEM((2, rows, line_len), f32),
            dma,
            dma((sections,)),
            dma((sections,)),
            dma((sections, per)),
            dma((steps,)),
            dma((2, steps)),
            dma((2, steps)),
            dma((steps,)),
            dma((sections, per)),
        ],
        compiler_params=pltpu.CompilerParams(
            collective_id=0, has_side_effects=True, vmem_limit_bytes=32 * 1024 * 1024
        ),
    )(
        surface, omegas, region_speed, fd_coeff, region_index, ref_region,
        jnp.asarray(weights), jnp.asarray(twiddle), jnp.asarray(kx),
    )


def solution(mesh):
    in_specs = (
        P(None, "shots", "strip", None),
        P(),
        P(),
        P(),
        P("depth", "strip", None),
        P("depth"),
    )
    out_specs = P("depth", "strip", "shots")
    run = functools.partial(shards, mesh.shape["depth"], mesh.shape["strip"])
    return jax.shard_map(run, mesh=mesh, in_specs=in_specs, out_specs=out_specs, check_vma=False)
```

```python
import functools
import math

import jax
import jax.numpy as jnp
import ml_dtypes
import numpy as np
from jax import lax
from jax.experimental import pallas as pl
from jax.experimental.pallas import tpu as pltpu
from jax.sharding import PartitionSpec as P

DAMPING = 0.05
LANES = 128
RADIX = 16
LEAD = 3
SQUARE_MAX = 9.5
MESH = pl.DeviceIdType.MESH


def fitted(function, terms):
    nodes = 0.5 * SQUARE_MAX * (1.0 - np.cos((np.arange(64) + 0.5) * np.pi / 64))
    fit = np.polynomial.Chebyshev.fit(nodes, function(np.sqrt(nodes)), terms - 1, domain=[0, SQUARE_MAX])
    return [float(c) for c in fit.convert(kind=np.polynomial.Polynomial).coef]


COS_TERMS = fitted(np.cos, 9)
SINC_TERMS = fitted(lambda x: np.sin(x) / x, 9)


def horner(terms, square):
    value = jnp.full(square.shape, terms[-1], jnp.float32)
    for term in reversed(terms[:-1]):
        value = value * square + term
    return value


def tables(line_len):
    inner = np.arange(LANES)
    outer = np.arange(RADIX)
    angle = 2.0 * np.pi * (inner[:, None] * inner[None, :] % LANES) / LANES
    cosine, sine = np.cos(angle), np.sin(angle)
    matrix = np.block([[cosine, -sine], [sine, cosine]])
    high = matrix.astype(ml_dtypes.bfloat16)
    low = (matrix - high.astype(np.float64)).astype(ml_dtypes.bfloat16)
    weights = np.concatenate([high, low]).astype(np.float32)
    twist = 2.0 * np.pi * (outer[:, None] * inner[None, :]) / line_len
    twiddle = np.stack([np.cos(twist), np.sin(twist)]).astype(np.float32)
    wave = outer[:, None] + RADIX * inner[None, :]
    signed = np.where(wave >= line_len // 2, wave - line_len, wave)
    kx = signed.astype(np.float32) * np.float32(2.0 * math.pi / line_len)
    return weights, twiddle, kx


def add(a, b):
    return a[0] + b[0], a[1] + b[1]


def sub(a, b):
    return a[0] - b[0], a[1] - b[1]


def times(a, c, s):
    return a[0] * c - a[1] * s, a[0] * s + a[1] * c


def dft4(z):
    even, odd = add(z[0], z[2]), add(z[1], z[3])
    p, r = sub(z[0], z[2]), sub(z[1], z[3])
    turned = (r[1], -r[0])
    return [add(even, odd), (p[0] + r[1], p[1] - r[0]), sub(even, odd), (p[0] - r[1], p[1] + r[0])]


def twist16(z, power):
    if power == 0:
        return z
    if power == 4:
        return z[1], -z[0]
    h = math.sqrt(0.5)
    if power == 2:
        return (z[0] + z[1]) * h, (z[1] - z[0]) * h
    if power == 6:
        return (z[1] - z[0]) * h, (z[0] + z[1]) * (-h)
    angle = -2.0 * math.pi * power / 16
    return times(z, math.cos(angle), math.sin(angle))


def dft16(z):
    mid = [[twist16(v, n * k) for k, v in enumerate(dft4([z[4 * m + n] for m in range(4)]))] for n in range(4)]
    out = [None] * 16
    for k in range(4):
        for j, v in enumerate(dft4([mid[n][k] for n in range(4)])):
            out[k + 4 * j] = v
    return out


def dft128(z, weights):
    stacked = jnp.concatenate(
        [jnp.concatenate([v[0] for v in z], 0), jnp.concatenate([v[1] for v in z], 0)], 1
    )
    high = stacked.astype(jnp.bfloat16)
    low = (stacked - high.astype(jnp.float32)).astype(jnp.bfloat16)
    wide = jnp.concatenate([high, low, high], 1)
    out = jnp.dot(wide, weights, preferred_element_type=jnp.float32)
    rows = z[0][0].shape[0]
    return [
        (out[c * rows:(c + 1) * rows, :LANES], out[c * rows:(c + 1) * rows, LANES:])
        for c in range(len(z))
    ]


def kernel(
    sections, strips, surface, omegas_in, speeds_in, coeffs_in, region, refs_in, weights_in, twiddle_in, kx_in,
    image,
    omegas, speeds, coeffs, refs, raw_weights, weights, twiddle, kx,
    wave, regions, ref_slow, ref_send, halo_out, halo_in, parts_out, parts_in, mult, phase, gain, gain_rows, partial,
    in_sem, ref_ssem, ref_rsem, reg_ssem, reg_rsem, halo_ssem, halo_rsem, img_ssem, img_rsem,
):
    me = lax.axis_index("depth")
    strip = lax.axis_index("strip")
    per = region.shape[0]
    steps = per * sections
    rows = region.shape[1]
    line_len = region.shape[2]
    chunks = line_len // LANES
    tile = (rows, LANES)
    region_count = speeds.shape[0]

    loads = [
        pltpu.make_async_copy(source, target, in_sem.at[n])
        for n, (source, target) in enumerate([
            (refs_in, refs), (speeds_in, speeds), (omegas_in, omegas), (coeffs_in, coeffs),
            (region, regions.at[pl.ds(me * per, per)]), (surface.at[:, me], wave),
            (twiddle_in, twiddle), (kx_in, kx), (weights_in, raw_weights),
        ])
    ]
    for load in loads:
        load.start()

    barrier = pltpu.get_barrier_semaphore()
    for delta in range(1, sections):
        pl.semaphore_signal(barrier, 1, device_id={"depth": lax.rem(me + delta, sections)}, device_id_type=MESH)

    @pl.when(strip > 0)
    def _():
        pl.semaphore_signal(barrier, 1, device_id={"strip": strip - 1}, device_id_type=MESH)

    @pl.when(strip < strips - 1)
    def _():
        pl.semaphore_signal(barrier, 1, device_id={"strip": strip + 1}, device_id_type=MESH)

    for load in loads[:4]:
        load.wait()
    row_no = lax.broadcasted_iota(jnp.int32, tile, 0)
    lane_no = lax.broadcasted_iota(jnp.int32, tile, 1)
    omega = jnp.zeros(tile, jnp.float32)
    for f in range(sections):
        omega = jnp.where(jnp.full(tile, me, jnp.int32) == f, omegas[f], omega)
    speed_rows = jnp.full(tile, 1.0, jnp.float32)
    coeff_rows = jnp.zeros(tile, jnp.float32)
    for r in range(region_count):
        speed_rows = jnp.where(row_no == r, speeds[r], speed_rows)
        coeff_rows = jnp.where(row_no == r, coeffs[r], coeff_rows)
    inv_rows = 1.0 / speed_rows
    gain_rows[...] = coeff_rows / omega
    for j in range(per):
        chosen = jnp.full(tile, refs[j], jnp.int32)
        speed_here = jnp.full(tile, 1.0, jnp.float32)
        for r in range(region_count):
            speed_here = jnp.where(chosen == r, speeds[r], speed_here)
        ref_send[j] = 1.0 / speed_here
        ref_slow[me * per + j] = 1.0 / speed_here

    @pl.when(strip == 0)
    def _():
        halo_in[0] = jnp.zeros(halo_in.shape[1:], jnp.float32)

    @pl.when(strip == strips - 1)
    def _():
        halo_in[1] = jnp.zeros(halo_in.shape[1:], jnp.float32)

    def ref_copy(delta):
        return pltpu.make_async_remote_copy(
            ref_send, ref_slow.at[pl.ds(me * per, per)], ref_ssem.at[delta], ref_rsem.at[me],
            device_id={"depth": lax.rem(me + delta, sections)}, device_id_type=MESH,
        )

    def region_copy(j, delta):
        return pltpu.make_async_remote_copy(
            regions.at[me * per + j], regions.at[me * per + j], reg_ssem.at[delta, j], reg_rsem.at[me * per + j],
            device_id={"depth": lax.rem(me + delta, sections)}, device_id_type=MESH,
        )

    def halo_copy(k, side):
        return pltpu.make_async_remote_copy(
            halo_out.at[side, k], halo_in.at[side, k], halo_ssem.at[side, k], halo_rsem.at[side, k],
            device_id={"strip": strip + 1 - 2 * side}, device_id_type=MESH,
        )

    def image_copy(k):
        return pltpu.make_async_remote_copy(
            parts_out.at[k], parts_in.at[me, lax.rem(k, per)], img_ssem.at[k], img_rsem.at[me, lax.rem(k, per)],
            device_id={"depth": k // per}, device_id_type=MESH,
        )

    pl.semaphore_wait(barrier, sections - 1 + jnp.minimum(strip, 1) + jnp.minimum(strips - 1 - strip, 1))

    for delta in range(1, sections):
        ref_copy(delta).start()

    def send_region(k):
        @pl.when(k // per == me)
        def _():
            for delta in range(1, sections):
                region_copy(lax.rem(k, per), delta).start()

    loads[4].wait()
    for k in range(LEAD):
        send_region(jnp.int32(k))
    for load in loads[5:]:
        load.wait()
    for block, source in enumerate((0, 0, 1)):
        weights[block * 2 * LANES:(block + 1) * 2 * LANES] = raw_weights[
            source * 2 * LANES:(source + 1) * 2 * LANES
        ].astype(jnp.bfloat16)
    for delta in range(1, sections):
        source = lax.rem(me + delta, sections)
        pltpu.make_async_remote_copy(
            ref_send, ref_slow.at[pl.ds(source * per, per)], ref_ssem.at[delta], ref_rsem.at[source],
            device_id={"depth": source}, device_id_type=MESH,
        ).wait_recv()

    def prepare(k, slot):
        ref = ref_slow[k]
        wave_ref = omega[:1] * ref[:1]
        excess = wave_ref * wave_ref - kx[...] * kx[...]
        root = jnp.sqrt(jnp.abs(excess))
        live = excess >= 0.0
        square = jnp.maximum(excess, 0.0)
        scale = 1.0 / line_len
        mult[0] = jnp.where(live, horner(COS_TERMS, square), jnp.exp(-root)) * scale
        mult[1] = jnp.where(live, root * horner(SINC_TERMS, square), 0.0) * scale
        angle = omega * (inv_rows - ref)
        square = angle * angle
        turn_cos = horner(COS_TERMS, square)
        turn_sin = angle * horner(SINC_TERMS, square)

        @pl.when(k // per != me)
        def _():
            pltpu.make_async_remote_copy(
                regions.at[k], regions.at[k], reg_ssem.at[0, 0], reg_rsem.at[k],
                device_id={"depth": me}, device_id_type=MESH,
            ).wait_recv()

        gains = gain_rows[...]
        spread = [
            [jnp.broadcast_to(t[r:r + 1], tile) for r in range(region_count)] for t in (turn_cos, turn_sin, gains)
        ]
        for a in range(chunks):
            cols = slice(a * LANES, (a + 1) * LANES)
            cells = regions[k, :, cols]
            masks = [(cells & bit) != 0 for bit in (1, 2, 4)]
            found = []
            for level in spread:
                for mask in masks:
                    level = [jnp.where(mask, level[2 * i + 1], level[2 * i]) for i in range(len(level) // 2)]
                found.append(level[0])
            phase[0, :, cols] = found[0]
            phase[1, :, cols] = found[1]
            gain[slot, :, cols] = found[2]

    prepare(jnp.int32(0), 0)

    def step(k, carry):
        slot = lax.rem(k, 2)

        @pl.when(k + LEAD < steps)
        def _():
            send_region(k + LEAD)

        def chunk(ref, *lead):
            return [ref[(*lead, slice(None), slice(a * LANES, (a + 1) * LANES))] for a in range(chunks)]

        z = list(zip(chunk(wave, 0), chunk(wave, 1)))
        z = dft16(z)
        twist = [(twiddle[0, c:c + 1], -twiddle[1, c:c + 1]) for c in range(chunks)]
        z = [z[0]] + [times(z[c], *twist[c]) for c in range(1, chunks)]
        z = dft128(z, weights[...])
        z = [times(z[c], mult[0, c:c + 1], mult[1, c:c + 1]) for c in range(chunks)]
        z = [(v[1], v[0]) for v in z]
        z = dft128(z, weights[...])
        z = [z[0]] + [times(z[c], *twist[c]) for c in range(1, chunks)]
        z = dft16(z)
        z = [(v[1], v[0]) for v in z]
        v = [times(z[a], pc, ps) for a, (pc, ps) in enumerate(zip(chunk(phase, 0), chunk(phase, 1)))]
        for a in range(chunks):
            for part in range(2):
                halo_out[0, k, part * chunks + a:part * chunks + a + 1] = v[a][part][rows - 1:]
                halo_out[1, k, part * chunks + a:part * chunks + a + 1] = v[a][part][:1]

        @pl.when(strip < strips - 1)
        def _():
            halo_copy(k, 0).start()

        @pl.when(strip > 0)
        def _():
            halo_copy(k, 1).start()

        lap = []
        for part in range(2):
            right = [pltpu.roll(v[a][part], 1, 1) for a in range(chunks)]
            left = [pltpu.roll(v[a][part], LANES - 1, 1) for a in range(chunks)]
            sums = []
            for a in range(chunks):
                here = v[a][part]
                before = jnp.where(lane_no == 0, right[a - 1], right[a])
                after = jnp.where(lane_no == LANES - 1, left[(a + 1) % chunks], left[a])
                above = jnp.where(row_no == 0, 0.0, pltpu.roll(here, 1, 0))
                below = jnp.where(row_no == rows - 1, 0.0, pltpu.roll(here, rows - 1, 0))
                sums.append(above + below + before + after - 4.0 * here)
            lap.append(sums)
        gains = chunk(gain, slot)
        for a in range(chunks):
            cols = slice(a * LANES, (a + 1) * LANES)
            lr, li = lap[0][a], lap[1][a]
            partial[0, :, cols] = v[a][0] + (DAMPING * lr - gains[a] * li)
            partial[1, :, cols] = v[a][1] + (gains[a] * lr + DAMPING * li)

        @pl.when(k + 1 < steps)
        def _():
            prepare(k + 1, 1 - slot)

        @pl.when(strip > 0)
        def _():
            halo_copy(k, 0).wait_recv()

        @pl.when(strip < strips - 1)
        def _():
            halo_copy(k, 1).wait_recv()

        gains = chunk(gain, slot)
        for a in range(chunks):
            cols = slice(a * LANES, (a + 1) * LANES)
            edge = []
            for part in range(2):
                at = part * chunks + a
                top = jnp.broadcast_to(halo_in[0, k, at:at + 1], tile)
                low = jnp.broadcast_to(halo_in[1, k, at:at + 1], tile)
                edge.append(jnp.where(row_no == 0, top, jnp.where(row_no == rows - 1, low, 0.0)))
            er, ei = edge
            new_re = partial[0, :, cols] + (DAMPING * er - gains[a] * ei)
            wave[0, :, cols] = new_re
            wave[1, :, cols] = partial[1, :, cols] + (gains[a] * er + DAMPING * ei)
            parts_out[k, :, cols] = new_re

        @pl.when(k // per != me)
        def _():
            image_copy(k).start()

        return carry

    lax.fori_loop(0, steps, step, 0)

    for j in range(per):
        for delta in range(1, sections):
            source = lax.rem(me + delta, sections)
            pltpu.make_async_remote_copy(
                parts_out.at[0], parts_in.at[source, j], img_ssem.at[0], img_rsem.at[source, j],
                device_id={"depth": source}, device_id_type=MESH,
            ).wait_recv()
        total = parts_out[me * per + j]
        for delta in range(1, sections):
            total = total + parts_in[lax.rem(me + delta, sections), j]
        image[j] = total

    for delta in range(1, sections):
        ref_copy(delta).wait_send()
        for j in range(per):
            region_copy(j, delta).wait_send()

    def drain(k, carry):
        @pl.when(k // per != me)
        def _():
            image_copy(k).wait_send()

        @pl.when(strip < strips - 1)
        def _():
            halo_copy(k, 0).wait_send()

        @pl.when(strip > 0)
        def _():
            halo_copy(k, 1).wait_send()

        return carry

    lax.fori_loop(0, steps, drain, 0)


def shards(sections, strips, surface, omegas, region_speed, fd_coeff, region_index, ref_region):
    freq_count, rows, line_len = surface.shape[1:]
    per = region_index.shape[0]
    steps = per * sections
    chunks = line_len // LANES
    assert freq_count == sections and chunks == RADIX
    weights, twiddle, kx = tables(line_len)
    f32 = jnp.float32
    vmem = pl.BlockSpec(memory_space=pltpu.VMEM)
    dma = pltpu.SemaphoreType.DMA
    return pl.pallas_call(
        functools.partial(kernel, sections, strips),
        out_shape=jax.ShapeDtypeStruct((per, rows, line_len), f32),
        in_specs=[pl.BlockSpec(memory_space=pltpu.HBM)] * 9,
        out_specs=vmem,
        scratch_shapes=[
            pltpu.SMEM(omegas.shape, f32),
            pltpu.SMEM(region_speed.shape, f32),
            pltpu.SMEM(fd_coeff.shape, f32),
            pltpu.SMEM(ref_region.shape, jnp.int32),
            pltpu.VMEM(weights.shape, f32),
            pltpu.VMEM((6 * LANES, 2 * LANES), jnp.bfloat16),
            pltpu.VMEM(twiddle.shape, f32),
            pltpu.VMEM(kx.shape, f32),
            pltpu.VMEM((2, rows, line_len), f32),
            pltpu.VMEM((steps, rows, line_len), jnp.int32),
            pltpu.VMEM((steps, rows, LANES), f32),
            pltpu.VMEM((per, rows, LANES), f32),
            pltpu.VMEM((2, steps, 2 * chunks, LANES), f32),
            pltpu.VMEM((2, steps, 2 * chunks, LANES), f32),
            pltpu.VMEM((steps, rows, line_len), f32),
            pltpu.VMEM((sections, per, rows, line_len), f32),
            pltpu.VMEM((2, chunks, LANES), f32),
            pltpu.VMEM((2, rows, line_len), f32),
            pltpu.VMEM((2, rows, line_len), f32),
            pltpu.VMEM((rows, LANES), f32),
            pltpu.VMEM((2, rows, line_len), f32),
            dma((9,)),
            dma((sections,)),
            dma((sections,)),
            dma((sections, per)),
            dma((steps,)),
            dma((2, steps)),
            dma((2, steps)),
            dma((steps,)),
            dma((sections, per)),
        ],
        compiler_params=pltpu.CompilerParams(
            collective_id=0, has_side_effects=True, vmem_limit_bytes=60 * 1024 * 1024
        ),
    )(
        surface, omegas, region_speed, fd_coeff, region_index, ref_region,
        jnp.asarray(weights), jnp.asarray(twiddle), jnp.asarray(kx),
    )


def solution(mesh):
    in_specs = (
        P(None, "shots", "strip", None),
        P(),
        P(),
        P(),
        P("depth", "strip", None),
        P("depth"),
    )
    out_specs = P("depth", "strip", "shots")
    run = functools.partial(shards, mesh.shape["depth"], mesh.shape["strip"])
    return jax.shard_map(run, mesh=mesh, in_specs=in_specs, out_specs=out_specs, check_vma=False)
```

```python
import functools
import math

import jax
import jax.numpy as jnp
import ml_dtypes
import numpy as np
from jax import lax
from jax.experimental import pallas as pl
from jax.experimental.pallas import tpu as pltpu
from jax.sharding import PartitionSpec as P

DAMPING = 0.05
LANES = 128
RADIX = 16
LEAD = 2
SQUARE_MAX = 9.5
MESH = pl.DeviceIdType.MESH


def fitted(function, terms):
    nodes = 0.5 * SQUARE_MAX * (1.0 - np.cos((np.arange(64) + 0.5) * np.pi / 64))
    fit = np.polynomial.Chebyshev.fit(nodes, function(np.sqrt(nodes)), terms - 1, domain=[0, SQUARE_MAX])
    return [float(c) for c in fit.convert(kind=np.polynomial.Polynomial).coef]


COS_TERMS = fitted(np.cos, 9)
SINC_TERMS = fitted(lambda x: np.sin(x) / x, 9)


def horner(terms, square):
    value = jnp.full(square.shape, terms[-1], jnp.float32)
    for term in reversed(terms[:-1]):
        value = value * square + term
    return value


def tables(line_len):
    inner = np.arange(LANES)
    outer = np.arange(RADIX)
    angle = 2.0 * np.pi * (inner[:, None] * inner[None, :] % LANES) / LANES
    cosine, sine = np.cos(angle), np.sin(angle)
    matrix = np.block([[cosine, -sine], [sine, cosine]])
    high = matrix.astype(ml_dtypes.bfloat16)
    low = (matrix - high.astype(np.float64)).astype(ml_dtypes.bfloat16)
    weights = np.concatenate([high, low]).astype(np.float32)
    twist = 2.0 * np.pi * (outer[:, None] * inner[None, :]) / line_len
    twiddle = np.stack([np.cos(twist), np.sin(twist)]).astype(np.float32)
    wave = outer[:, None] + RADIX * inner[None, :]
    signed = np.where(wave >= line_len // 2, wave - line_len, wave)
    kx = signed.astype(np.float32) * np.float32(2.0 * math.pi / line_len)
    return weights, twiddle, kx


def add(a, b):
    return a[0] + b[0], a[1] + b[1]


def sub(a, b):
    return a[0] - b[0], a[1] - b[1]


def times(a, c, s):
    return a[0] * c - a[1] * s, a[0] * s + a[1] * c


def dft4(z):
    even, odd = add(z[0], z[2]), add(z[1], z[3])
    p, r = sub(z[0], z[2]), sub(z[1], z[3])
    turned = (r[1], -r[0])
    return [add(even, odd), (p[0] + r[1], p[1] - r[0]), sub(even, odd), (p[0] - r[1], p[1] + r[0])]


def twist16(z, power):
    if power == 0:
        return z
    if power == 4:
        return z[1], -z[0]
    h = math.sqrt(0.5)
    if power == 2:
        return (z[0] + z[1]) * h, (z[1] - z[0]) * h
    if power == 6:
        return (z[1] - z[0]) * h, (z[0] + z[1]) * (-h)
    angle = -2.0 * math.pi * power / 16
    return times(z, math.cos(angle), math.sin(angle))


def dft16(z):
    mid = [[twist16(v, n * k) for k, v in enumerate(dft4([z[4 * m + n] for m in range(4)]))] for n in range(4)]
    out = [None] * 16
    for k in range(4):
        for j, v in enumerate(dft4([mid[n][k] for n in range(4)])):
            out[k + 4 * j] = v
    return out


def dft128(z, weights):
    stacked = jnp.concatenate(
        [jnp.concatenate([v[0] for v in z], 0), jnp.concatenate([v[1] for v in z], 0)], 1
    )
    high = stacked.astype(jnp.bfloat16)
    low = (stacked - high.astype(jnp.float32)).astype(jnp.bfloat16)
    wide = jnp.concatenate([high, low, high], 1)
    out = jnp.dot(wide, weights, preferred_element_type=jnp.float32)
    rows = z[0][0].shape[0]
    return [
        (out[c * rows:(c + 1) * rows, :LANES], out[c * rows:(c + 1) * rows, LANES:])
        for c in range(len(z))
    ]


def kernel(
    sections, strips, surface, omegas_in, speeds_in, coeffs_in, region, refs_in, weights_in, twiddle_in, kx_in,
    image,
    omegas, speeds, coeffs, refs, raw_weights, weights, twiddle, kx,
    wave, regions, ref_slow, ref_send, halo_out, halo_in, parts_out, parts_in, mult, phase, gain, gain_rows, partial,
    in_sem, ref_ssem, ref_rsem, reg_ssem, reg_rsem, halo_ssem, halo_rsem, img_ssem, img_rsem,
):
    me = lax.axis_index("depth")
    strip = lax.axis_index("strip")
    per = region.shape[0]
    steps = per * sections
    rows = region.shape[1]
    line_len = region.shape[2]
    chunks = line_len // LANES
    tile = (rows, LANES)
    region_count = speeds.shape[0]

    loads = [
        pltpu.make_async_copy(source, target, in_sem.at[n])
        for n, (source, target) in enumerate([
            (refs_in, refs), (speeds_in, speeds), (omegas_in, omegas), (coeffs_in, coeffs),
            (region, regions.at[pl.ds(me * per, per)]), (surface.at[:, me], wave),
            (twiddle_in, twiddle), (kx_in, kx), (weights_in, raw_weights),
        ])
    ]
    for load in loads:
        load.start()

    barrier = pltpu.get_barrier_semaphore()
    for delta in range(1, sections):
        pl.semaphore_signal(barrier, 1, device_id={"depth": lax.rem(me + delta, sections)}, device_id_type=MESH)

    @pl.when(strip > 0)
    def _():
        pl.semaphore_signal(barrier, 1, device_id={"strip": strip - 1}, device_id_type=MESH)

    @pl.when(strip < strips - 1)
    def _():
        pl.semaphore_signal(barrier, 1, device_id={"strip": strip + 1}, device_id_type=MESH)

    for load in loads[:4]:
        load.wait()
    row_no = lax.broadcasted_iota(jnp.int32, tile, 0)
    lane_no = lax.broadcasted_iota(jnp.int32, tile, 1)
    omega = jnp.zeros(tile, jnp.float32)
    for f in range(sections):
        omega = jnp.where(jnp.full(tile, me, jnp.int32) == f, omegas[f], omega)
    speed_rows = jnp.full(tile, 1.0, jnp.float32)
    coeff_rows = jnp.zeros(tile, jnp.float32)
    for r in range(region_count):
        speed_rows = jnp.where(row_no == r, speeds[r], speed_rows)
        coeff_rows = jnp.where(row_no == r, coeffs[r], coeff_rows)
    inv_rows = 1.0 / speed_rows
    gain_rows[...] = coeff_rows / omega
    for j in range(per):
        chosen = jnp.full(tile, refs[j], jnp.int32)
        speed_here = jnp.full(tile, 1.0, jnp.float32)
        for r in range(region_count):
            speed_here = jnp.where(chosen == r, speeds[r], speed_here)
        ref_send[j] = 1.0 / speed_here
        ref_slow[me * per + j] = 1.0 / speed_here

    @pl.when(strip == 0)
    def _():
        halo_in[0] = jnp.zeros(halo_in.shape[1:], jnp.float32)

    @pl.when(strip == strips - 1)
    def _():
        halo_in[1] = jnp.zeros(halo_in.shape[1:], jnp.float32)

    def ref_copy(delta):
        return pltpu.make_async_remote_copy(
            ref_send, ref_slow.at[pl.ds(me * per, per)], ref_ssem.at[delta], ref_rsem.at[me],
            device_id={"depth": lax.rem(me + delta, sections)}, device_id_type=MESH,
        )

    def region_copy(j, delta):
        return pltpu.make_async_remote_copy(
            regions.at[me * per + j], regions.at[me * per + j], reg_ssem.at[delta, j], reg_rsem.at[me * per + j],
            device_id={"depth": lax.rem(me + delta, sections)}, device_id_type=MESH,
        )

    def halo_copy(k, side):
        return pltpu.make_async_remote_copy(
            halo_out.at[side, k], halo_in.at[side, k], halo_ssem.at[side, k], halo_rsem.at[side, k],
            device_id={"strip": strip + 1 - 2 * side}, device_id_type=MESH,
        )

    def image_copy(k):
        return pltpu.make_async_remote_copy(
            parts_out.at[k], parts_in.at[me, lax.rem(k, per)], img_ssem.at[k], img_rsem.at[me, lax.rem(k, per)],
            device_id={"depth": k // per}, device_id_type=MESH,
        )

    pl.semaphore_wait(barrier, sections - 1 + jnp.minimum(strip, 1) + jnp.minimum(strips - 1 - strip, 1))

    for delta in range(1, sections):
        ref_copy(delta).start()

    def send_region(k):
        @pl.when(k // per == me)
        def _():
            for delta in range(1, sections):
                region_copy(lax.rem(k, per), delta).start()

    loads[4].wait()
    for k in range(LEAD):
        send_region(jnp.int32(k))
    for load in loads[5:]:
        load.wait()
    for block, source in enumerate((0, 0, 1)):
        weights[block * 2 * LANES:(block + 1) * 2 * LANES] = raw_weights[
            source * 2 * LANES:(source + 1) * 2 * LANES
        ].astype(jnp.bfloat16)
    for delta in range(1, sections):
        source = lax.rem(me + delta, sections)
        pltpu.make_async_remote_copy(
            ref_send, ref_slow.at[pl.ds(source * per, per)], ref_ssem.at[delta], ref_rsem.at[source],
            device_id={"depth": source}, device_id_type=MESH,
        ).wait_recv()

    def prepare(k, slot):
        ref = ref_slow[k]
        wave_ref = omega[:1] * ref[:1]
        excess = wave_ref * wave_ref - kx[...] * kx[...]
        root = jnp.sqrt(jnp.abs(excess))
        live = excess >= 0.0
        square = jnp.maximum(excess, 0.0)
        scale = 1.0 / line_len
        mult[0] = jnp.where(live, horner(COS_TERMS, square), jnp.exp(-root)) * scale
        mult[1] = jnp.where(live, root * horner(SINC_TERMS, square), 0.0) * scale
        angle = omega * (inv_rows - ref)
        square = angle * angle
        turn_cos = horner(COS_TERMS, square)
        turn_sin = angle * horner(SINC_TERMS, square)

        @pl.when(k // per != me)
        def _():
            pltpu.make_async_remote_copy(
                regions.at[k], regions.at[k], reg_ssem.at[0, 0], reg_rsem.at[k],
                device_id={"depth": me}, device_id_type=MESH,
            ).wait_recv()

        gains = gain_rows[...]
        spread = [
            [jnp.broadcast_to(t[r:r + 1], tile) for r in range(region_count)] for t in (turn_cos, turn_sin, gains)
        ]
        for a in range(chunks):
            cols = slice(a * LANES, (a + 1) * LANES)
            cells = regions[k, :, cols]
            masks = [(cells & bit) != 0 for bit in (1, 2, 4)]
            found = []
            for level in spread:
                for mask in masks:
                    level = [jnp.where(mask, level[2 * i + 1], level[2 * i]) for i in range(len(level) // 2)]
                found.append(level[0])
            phase[0, :, cols] = found[0]
            phase[1, :, cols] = found[1]
            gain[slot, :, cols] = found[2]

    prepare(jnp.int32(0), 0)

    def step(k, carry):
        slot = lax.rem(k, 2)

        def chunk(ref, *lead):
            return [ref[(*lead, slice(None), slice(a * LANES, (a + 1) * LANES))] for a in range(chunks)]

        z = list(zip(chunk(wave, 0), chunk(wave, 1)))
        z = dft16(z)
        twist = [(twiddle[0, c:c + 1], -twiddle[1, c:c + 1]) for c in range(chunks)]
        z = [z[0]] + [times(z[c], *twist[c]) for c in range(1, chunks)]
        z = dft128(z, weights[...])
        z = [times(z[c], mult[0, c:c + 1], mult[1, c:c + 1]) for c in range(chunks)]
        z = [(v[1], v[0]) for v in z]
        z = dft128(z, weights[...])
        z = [z[0]] + [times(z[c], *twist[c]) for c in range(1, chunks)]
        z = dft16(z)
        z = [(v[1], v[0]) for v in z]
        v = [times(z[a], pc, ps) for a, (pc, ps) in enumerate(zip(chunk(phase, 0), chunk(phase, 1)))]
        for a in range(chunks):
            for part in range(2):
                halo_out[0, k, part * chunks + a:part * chunks + a + 1] = v[a][part][rows - 1:]
                halo_out[1, k, part * chunks + a:part * chunks + a + 1] = v[a][part][:1]

        @pl.when(strip < strips - 1)
        def _():
            halo_copy(k, 0).start()

        @pl.when(strip > 0)
        def _():
            halo_copy(k, 1).start()

        @pl.when(k + LEAD < steps)
        def _():
            send_region(k + LEAD)

        @pl.when((k > 0) & ((k - 1) // per != me))
        def _():
            image_copy(k - 1).start()

        lap = []
        for part in range(2):
            right = [pltpu.roll(v[a][part], 1, 1) for a in range(chunks)]
            left = [pltpu.roll(v[a][part], LANES - 1, 1) for a in range(chunks)]
            sums = []
            for a in range(chunks):
                here = v[a][part]
                before = jnp.where(lane_no == 0, right[a - 1], right[a])
                after = jnp.where(lane_no == LANES - 1, left[(a + 1) % chunks], left[a])
                above = jnp.where(row_no == 0, 0.0, pltpu.roll(here, 1, 0))
                below = jnp.where(row_no == rows - 1, 0.0, pltpu.roll(here, rows - 1, 0))
                sums.append(above + below + before + after - 4.0 * here)
            lap.append(sums)
        gains = chunk(gain, slot)
        for a in range(chunks):
            cols = slice(a * LANES, (a + 1) * LANES)
            lr, li = lap[0][a], lap[1][a]
            partial[0, :, cols] = v[a][0] + (DAMPING * lr - gains[a] * li)
            partial[1, :, cols] = v[a][1] + (gains[a] * lr + DAMPING * li)

        @pl.when(k + 1 < steps)
        def _():
            prepare(k + 1, 1 - slot)

        @pl.when(strip > 0)
        def _():
            halo_copy(k, 0).wait_recv()

        @pl.when(strip < strips - 1)
        def _():
            halo_copy(k, 1).wait_recv()

        gains = chunk(gain, slot)
        for a in range(chunks):
            cols = slice(a * LANES, (a + 1) * LANES)
            edge = []
            for part in range(2):
                at = part * chunks + a
                top = jnp.broadcast_to(halo_in[0, k, at:at + 1], tile)
                low = jnp.broadcast_to(halo_in[1, k, at:at + 1], tile)
                edge.append(jnp.where(row_no == 0, top, jnp.where(row_no == rows - 1, low, 0.0)))
            er, ei = edge
            new_re = partial[0, :, cols] + (DAMPING * er - gains[a] * ei)
            wave[0, :, cols] = new_re
            wave[1, :, cols] = partial[1, :, cols] + (gains[a] * er + DAMPING * ei)
            parts_out[k, :, cols] = new_re

        return carry

    lax.fori_loop(0, steps, step, 0)

    @pl.when(me < sections - 1)
    def _():
        image_copy(jnp.int32(steps - 1)).start()

    for j in range(per):
        for delta in range(1, sections):
            source = lax.rem(me + delta, sections)
            pltpu.make_async_remote_copy(
                parts_out.at[0], parts_in.at[source, j], img_ssem.at[0], img_rsem.at[source, j],
                device_id={"depth": source}, device_id_type=MESH,
            ).wait_recv()
        total = parts_out[me * per + j]
        for delta in range(1, sections):
            total = total + parts_in[lax.rem(me + delta, sections), j]
        image[j] = total

    for delta in range(1, sections):
        ref_copy(delta).wait_send()
        for j in range(per):
            region_copy(j, delta).wait_send()

    def drain(k, carry):
        @pl.when(k // per != me)
        def _():
            image_copy(k).wait_send()

        @pl.when(strip < strips - 1)
        def _():
            halo_copy(k, 0).wait_send()

        @pl.when(strip > 0)
        def _():
            halo_copy(k, 1).wait_send()

        return carry

    lax.fori_loop(0, steps, drain, 0)


def shards(sections, strips, surface, omegas, region_speed, fd_coeff, region_index, ref_region):
    freq_count, rows, line_len = surface.shape[1:]
    per = region_index.shape[0]
    steps = per * sections
    chunks = line_len // LANES
    assert freq_count == sections and chunks == RADIX
    weights, twiddle, kx = tables(line_len)
    f32 = jnp.float32
    vmem = pl.BlockSpec(memory_space=pltpu.VMEM)
    dma = pltpu.SemaphoreType.DMA
    return pl.pallas_call(
        functools.partial(kernel, sections, strips),
        out_shape=jax.ShapeDtypeStruct((per, rows, line_len), f32),
        in_specs=[pl.BlockSpec(memory_space=pltpu.HBM)] * 9,
        out_specs=vmem,
        scratch_shapes=[
            pltpu.SMEM(omegas.shape, f32),
            pltpu.SMEM(region_speed.shape, f32),
            pltpu.SMEM(fd_coeff.shape, f32),
            pltpu.SMEM(ref_region.shape, jnp.int32),
            pltpu.VMEM(weights.shape, f32),
            pltpu.VMEM((6 * LANES, 2 * LANES), jnp.bfloat16),
            pltpu.VMEM(twiddle.shape, f32),
            pltpu.VMEM(kx.shape, f32),
            pltpu.VMEM((2, rows, line_len), f32),
            pltpu.VMEM((steps, rows, line_len), jnp.int32),
            pltpu.VMEM((steps, rows, LANES), f32),
            pltpu.VMEM((per, rows, LANES), f32),
            pltpu.VMEM((2, steps, 2 * chunks, LANES), f32),
            pltpu.VMEM((2, steps, 2 * chunks, LANES), f32),
            pltpu.VMEM((steps, rows, line_len), f32),
            pltpu.VMEM((sections, per, rows, line_len), f32),
            pltpu.VMEM((2, chunks, LANES), f32),
            pltpu.VMEM((2, rows, line_len), f32),
            pltpu.VMEM((2, rows, line_len), f32),
            pltpu.VMEM((rows, LANES), f32),
            pltpu.VMEM((2, rows, line_len), f32),
            dma((9,)),
            dma((sections,)),
            dma((sections,)),
            dma((sections, per)),
            dma((steps,)),
            dma((2, steps)),
            dma((2, steps)),
            dma((steps,)),
            dma((sections, per)),
        ],
        compiler_params=pltpu.CompilerParams(
            collective_id=0, has_side_effects=True, vmem_limit_bytes=60 * 1024 * 1024
        ),
    )(
        surface, omegas, region_speed, fd_coeff, region_index, ref_region,
        jnp.asarray(weights), jnp.asarray(twiddle), jnp.asarray(kx),
    )


def solution(mesh):
    in_specs = (
        P(None, "shots", "strip", None),
        P(),
        P(),
        P(),
        P("depth", "strip", None),
        P("depth"),
    )
    out_specs = P("depth", "strip", "shots")
    run = functools.partial(shards, mesh.shape["depth"], mesh.shape["strip"])
    return jax.shard_map(run, mesh=mesh, in_specs=in_specs, out_specs=out_specs, check_vma=False)
```

```python
import functools
import math

import jax
import jax.numpy as jnp
import ml_dtypes
import numpy as np
from jax import lax
from jax.experimental import pallas as pl
from jax.experimental.pallas import tpu as pltpu
from jax.sharding import PartitionSpec as P

DAMPING = 0.05
LANES = 128
RADIX = 16
LEAD = 3
DIRECT = 2
SQUARE_MAX = 9.5
MESH = pl.DeviceIdType.MESH


def fitted(function, terms):
    nodes = 0.5 * SQUARE_MAX * (1.0 - np.cos((np.arange(64) + 0.5) * np.pi / 64))
    fit = np.polynomial.Chebyshev.fit(nodes, function(np.sqrt(nodes)), terms - 1, domain=[0, SQUARE_MAX])
    return [float(c) for c in fit.convert(kind=np.polynomial.Polynomial).coef]


COS_TERMS = fitted(np.cos, 9)
SINC_TERMS = fitted(lambda x: np.sin(x) / x, 9)


def horner(terms, square):
    value = jnp.full(square.shape, terms[-1], jnp.float32)
    for term in reversed(terms[:-1]):
        value = value * square + term
    return value


def tables(line_len):
    inner = np.arange(LANES)
    outer = np.arange(RADIX)
    angle = 2.0 * np.pi * (inner[:, None] * inner[None, :] % LANES) / LANES
    cosine, sine = np.cos(angle), np.sin(angle)
    matrix = np.block([[cosine, -sine], [sine, cosine]])
    high = matrix.astype(ml_dtypes.bfloat16)
    low = (matrix - high.astype(np.float64)).astype(ml_dtypes.bfloat16)
    weights = np.concatenate([high, low]).astype(np.float32)
    twist = 2.0 * np.pi * (outer[:, None] * inner[None, :]) / line_len
    twiddle = np.stack([np.cos(twist), np.sin(twist)]).astype(np.float32)
    wave = outer[:, None] + RADIX * inner[None, :]
    signed = np.where(wave >= line_len // 2, wave - line_len, wave)
    kx = signed.astype(np.float32) * np.float32(2.0 * math.pi / line_len)
    return weights, twiddle, kx


def add(a, b):
    return a[0] + b[0], a[1] + b[1]


def sub(a, b):
    return a[0] - b[0], a[1] - b[1]


def times(a, c, s):
    return a[0] * c - a[1] * s, a[0] * s + a[1] * c


def dft4(z):
    even, odd = add(z[0], z[2]), add(z[1], z[3])
    p, r = sub(z[0], z[2]), sub(z[1], z[3])
    turned = (r[1], -r[0])
    return [add(even, odd), (p[0] + r[1], p[1] - r[0]), sub(even, odd), (p[0] - r[1], p[1] + r[0])]


def twist16(z, power):
    if power == 0:
        return z
    if power == 4:
        return z[1], -z[0]
    h = math.sqrt(0.5)
    if power == 2:
        return (z[0] + z[1]) * h, (z[1] - z[0]) * h
    if power == 6:
        return (z[1] - z[0]) * h, (z[0] + z[1]) * (-h)
    angle = -2.0 * math.pi * power / 16
    return times(z, math.cos(angle), math.sin(angle))


def dft16(z):
    mid = [[twist16(v, n * k) for k, v in enumerate(dft4([z[4 * m + n] for m in range(4)]))] for n in range(4)]
    out = [None] * 16
    for k in range(4):
        for j, v in enumerate(dft4([mid[n][k] for n in range(4)])):
            out[k + 4 * j] = v
    return out


def dft128(z, weights):
    stacked = jnp.concatenate(
        [jnp.concatenate([v[0] for v in z], 0), jnp.concatenate([v[1] for v in z], 0)], 1
    )
    high = stacked.astype(jnp.bfloat16)
    low = (stacked - high.astype(jnp.float32)).astype(jnp.bfloat16)
    wide = jnp.concatenate([high, low, high], 1)
    out = jnp.dot(wide, weights, preferred_element_type=jnp.float32)
    rows = z[0][0].shape[0]
    return [
        (out[c * rows:(c + 1) * rows, :LANES], out[c * rows:(c + 1) * rows, LANES:])
        for c in range(len(z))
    ]


def kernel(
    sections, strips, surface, omegas_in, speeds_in, coeffs_in, region, refs_in, weights_in, twiddle_in, kx_in,
    image,
    omegas, speeds, coeffs, refs, raw_weights, weights, twiddle, kx,
    wave, regions, ref_slow, ref_send, halo_out, halo_in, parts_out, near_in, across_out, across_in, diagonal_in, mult, phase, gain, gain_rows, partial,
    in_sem, ref_ssem, ref_rsem, reg_ssem, reg_rsem, halo_ssem, halo_rsem, img_ssem, near_rsem, across_ssem, across_rsem, diagonal_rsem,
):
    me = lax.axis_index("depth")
    strip = lax.axis_index("strip")
    per = region.shape[0]
    steps = per * sections
    rows = region.shape[1]
    line_len = region.shape[2]
    chunks = line_len // LANES
    tile = (rows, LANES)
    region_count = speeds.shape[0]

    loads = [
        pltpu.make_async_copy(source, target, in_sem.at[n])
        for n, (source, target) in enumerate([
            (refs_in, refs), (speeds_in, speeds), (omegas_in, omegas), (coeffs_in, coeffs),
            (region, regions.at[pl.ds(me * per, per)]), (surface.at[:, me], wave),
            (twiddle_in, twiddle), (kx_in, kx), (weights_in, raw_weights),
        ])
    ]
    for load in loads:
        load.start()

    barrier = pltpu.get_barrier_semaphore()
    for delta in range(1, sections):
        pl.semaphore_signal(barrier, 1, device_id={"depth": lax.rem(me + delta, sections)}, device_id_type=MESH)

    @pl.when(strip > 0)
    def _():
        pl.semaphore_signal(barrier, 1, device_id={"strip": strip - 1}, device_id_type=MESH)

    @pl.when(strip < strips - 1)
    def _():
        pl.semaphore_signal(barrier, 1, device_id={"strip": strip + 1}, device_id_type=MESH)

    for load in loads[:4]:
        load.wait()
    row_no = lax.broadcasted_iota(jnp.int32, tile, 0)
    lane_no = lax.broadcasted_iota(jnp.int32, tile, 1)
    omega = jnp.zeros(tile, jnp.float32)
    for f in range(sections):
        omega = jnp.where(jnp.full(tile, me, jnp.int32) == f, omegas[f], omega)
    speed_rows = jnp.full(tile, 1.0, jnp.float32)
    coeff_rows = jnp.zeros(tile, jnp.float32)
    for r in range(region_count):
        speed_rows = jnp.where(row_no == r, speeds[r], speed_rows)
        coeff_rows = jnp.where(row_no == r, coeffs[r], coeff_rows)
    inv_rows = 1.0 / speed_rows
    gain_rows[...] = coeff_rows / omega
    for j in range(per):
        chosen = jnp.full(tile, refs[j], jnp.int32)
        speed_here = jnp.full(tile, 1.0, jnp.float32)
        for r in range(region_count):
            speed_here = jnp.where(chosen == r, speeds[r], speed_here)
        ref_send[j] = 1.0 / speed_here
        ref_slow[me * per + j] = 1.0 / speed_here

    @pl.when(strip == 0)
    def _():
        halo_in[0] = jnp.zeros(halo_in.shape[1:], jnp.float32)

    @pl.when(strip == strips - 1)
    def _():
        halo_in[1] = jnp.zeros(halo_in.shape[1:], jnp.float32)

    def ref_copy(delta):
        return pltpu.make_async_remote_copy(
            ref_send, ref_slow.at[pl.ds(me * per, per)], ref_ssem.at[delta], ref_rsem.at[me],
            device_id={"depth": lax.rem(me + delta, sections)}, device_id_type=MESH,
        )

    def partner(d):
        return d + 1 - 2 * lax.rem(d, 2)

    def across(d):
        return lax.rem(d + 2, sections)

    def region_copy(k, target, way):
        return pltpu.make_async_remote_copy(
            regions.at[k], regions.at[k], reg_ssem.at[way, k], reg_rsem.at[k],
            device_id={"depth": target}, device_id_type=MESH,
        )

    def halo_copy(k, side):
        return pltpu.make_async_remote_copy(
            halo_out.at[side, k], halo_in.at[side, k], halo_ssem.at[side, k], halo_rsem.at[side, k],
            device_id={"strip": strip + 1 - 2 * side}, device_id_type=MESH,
        )

    def near_copy(k):
        return pltpu.make_async_remote_copy(
            parts_out.at[k], near_in.at[k // per // 2, lax.rem(k, per)], img_ssem.at[k],
            near_rsem.at[k // per // 2, lax.rem(k, per)],
            device_id={"depth": partner(me)}, device_id_type=MESH,
        )

    def diagonal_copy(k):
        return pltpu.make_async_remote_copy(
            parts_out.at[k], diagonal_in.at[k - (steps - DIRECT)], img_ssem.at[k],
            diagonal_rsem.at[k - (steps - DIRECT)],
            device_id={"depth": k // per}, device_id_type=MESH,
        )

    def across_copy(k):
        return pltpu.make_async_remote_copy(
            across_out.at[lax.rem(k, per)], across_in.at[lax.rem(k, per)], across_ssem.at[lax.rem(k, per)],
            across_rsem.at[lax.rem(k, per)],
            device_id={"depth": k // per}, device_id_type=MESH,
        )

    def is_near(k):
        owner = k // per
        return (me == partner(owner)) | ((me == partner(across(owner))) & (k < steps - DIRECT))

    def is_diagonal(k):
        return (me == partner(across(k // per))) & (k >= steps - DIRECT)

    def is_across(k):
        return me == across(k // per)

    def send_part(k):
        @pl.when(is_near(k))
        def _():
            near_copy(k).start()

        @pl.when(is_diagonal(k))
        def _():
            diagonal_copy(k).start()

    def send_sum(k):
        @pl.when(is_across(k))
        def _():
            j = lax.rem(k, per)

            @pl.when(k < steps - DIRECT)
            def _():
                near_copy(k).wait_recv()
                across_out[j] = parts_out[k] + near_in[k // per // 2, j]

            @pl.when(k >= steps - DIRECT)
            def _():
                across_out[j] = parts_out[k]

            across_copy(k).start()

    pl.semaphore_wait(barrier, sections - 1 + jnp.minimum(strip, 1) + jnp.minimum(strips - 1 - strip, 1))

    for delta in range(1, sections):
        ref_copy(delta).start()

    def send_region(k):
        owner = k // per

        @pl.when(owner == me)
        def _():
            region_copy(k, across(me), 0).start()

            @pl.when(k < DIRECT)
            def _():
                region_copy(k, partner(across(me)), 2).start()

            region_copy(k, partner(me), 1).start()

    def relay_region(k):
        @pl.when(is_across(k))
        def _():
            region_copy(k, partner(me), 1).wait_recv()
            region_copy(k, partner(me), 1).start()

    loads[4].wait()
    for k in range(LEAD):
        send_region(jnp.int32(k))
    for load in loads[5:]:
        load.wait()
    for block, source in enumerate((0, 0, 1)):
        weights[block * 2 * LANES:(block + 1) * 2 * LANES] = raw_weights[
            source * 2 * LANES:(source + 1) * 2 * LANES
        ].astype(jnp.bfloat16)
    for delta in range(1, sections):
        source = lax.rem(me + delta, sections)
        pltpu.make_async_remote_copy(
            ref_send, ref_slow.at[pl.ds(source * per, per)], ref_ssem.at[delta], ref_rsem.at[source],
            device_id={"depth": source}, device_id_type=MESH,
        ).wait_recv()

    def prepare(k, slot):
        ref = ref_slow[k]
        wave_ref = omega[:1] * ref[:1]
        excess = wave_ref * wave_ref - kx[...] * kx[...]
        root = jnp.sqrt(jnp.abs(excess))
        live = excess >= 0.0
        square = jnp.maximum(excess, 0.0)
        scale = 1.0 / line_len
        mult[0] = jnp.where(live, horner(COS_TERMS, square), jnp.exp(-root)) * scale
        mult[1] = jnp.where(live, root * horner(SINC_TERMS, square), 0.0) * scale
        angle = omega * (inv_rows - ref)
        square = angle * angle
        turn_cos = horner(COS_TERMS, square)
        turn_sin = angle * horner(SINC_TERMS, square)

        @pl.when((k // per != me) & jnp.logical_not(is_across(k) & (k >= DIRECT)))
        def _():
            region_copy(k, me, 0).wait_recv()

        gains = gain_rows[...]
        spread = [
            [jnp.broadcast_to(t[r:r + 1], tile) for r in range(region_count)] for t in (turn_cos, turn_sin, gains)
        ]
        for a in range(chunks):
            cols = slice(a * LANES, (a + 1) * LANES)
            cells = regions[k, :, cols]
            masks = [(cells & bit) != 0 for bit in (1, 2, 4)]
            found = []
            for level in spread:
                for mask in masks:
                    level = [jnp.where(mask, level[2 * i + 1], level[2 * i]) for i in range(len(level) // 2)]
                found.append(level[0])
            phase[0, :, cols] = found[0]
            phase[1, :, cols] = found[1]
            gain[slot, :, cols] = found[2]

    prepare(jnp.int32(0), 0)

    def step(k, carry):
        slot = lax.rem(k, 2)

        def chunk(ref, *lead):
            return [ref[(*lead, slice(None), slice(a * LANES, (a + 1) * LANES))] for a in range(chunks)]

        z = list(zip(chunk(wave, 0), chunk(wave, 1)))
        z = dft16(z)
        twist = [(twiddle[0, c:c + 1], -twiddle[1, c:c + 1]) for c in range(chunks)]
        z = [z[0]] + [times(z[c], *twist[c]) for c in range(1, chunks)]
        z = dft128(z, weights[...])
        z = [times(z[c], mult[0, c:c + 1], mult[1, c:c + 1]) for c in range(chunks)]
        z = [(v[1], v[0]) for v in z]
        z = dft128(z, weights[...])
        z = [z[0]] + [times(z[c], *twist[c]) for c in range(1, chunks)]
        z = dft16(z)
        z = [(v[1], v[0]) for v in z]
        v = [times(z[a], pc, ps) for a, (pc, ps) in enumerate(zip(chunk(phase, 0), chunk(phase, 1)))]
        for a in range(chunks):
            for part in range(2):
                halo_out[0, k, part * chunks + a:part * chunks + a + 1] = v[a][part][rows - 1:]
                halo_out[1, k, part * chunks + a:part * chunks + a + 1] = v[a][part][:1]

        @pl.when(strip < strips - 1)
        def _():
            halo_copy(k, 0).start()

        @pl.when(strip > 0)
        def _():
            halo_copy(k, 1).start()

        @pl.when(k + LEAD < steps)
        def _():
            send_region(k + LEAD)

        @pl.when(k + DIRECT < steps)
        def _():
            relay_region(k + DIRECT)

        @pl.when(k > 0)
        def _():
            send_part(k - 1)

        @pl.when(k > 1)
        def _():
            send_sum(k - 2)

        lap = []
        for part in range(2):
            right = [pltpu.roll(v[a][part], 1, 1) for a in range(chunks)]
            left = [pltpu.roll(v[a][part], LANES - 1, 1) for a in range(chunks)]
            sums = []
            for a in range(chunks):
                here = v[a][part]
                before = jnp.where(lane_no == 0, right[a - 1], right[a])
                after = jnp.where(lane_no == LANES - 1, left[(a + 1) % chunks], left[a])
                above = jnp.where(row_no == 0, 0.0, pltpu.roll(here, 1, 0))
                below = jnp.where(row_no == rows - 1, 0.0, pltpu.roll(here, rows - 1, 0))
                sums.append(above + below + before + after - 4.0 * here)
            lap.append(sums)
        gains = chunk(gain, slot)
        for a in range(chunks):
            cols = slice(a * LANES, (a + 1) * LANES)
            lr, li = lap[0][a], lap[1][a]
            partial[0, :, cols] = v[a][0] + (DAMPING * lr - gains[a] * li)
            partial[1, :, cols] = v[a][1] + (gains[a] * lr + DAMPING * li)

        @pl.when(k + 1 < steps)
        def _():
            prepare(k + 1, 1 - slot)

        @pl.when(strip > 0)
        def _():
            halo_copy(k, 0).wait_recv()

        @pl.when(strip < strips - 1)
        def _():
            halo_copy(k, 1).wait_recv()

        gains = chunk(gain, slot)
        for a in range(chunks):
            cols = slice(a * LANES, (a + 1) * LANES)
            edge = []
            for part in range(2):
                at = part * chunks + a
                top = jnp.broadcast_to(halo_in[0, k, at:at + 1], tile)
                low = jnp.broadcast_to(halo_in[1, k, at:at + 1], tile)
                edge.append(jnp.where(row_no == 0, top, jnp.where(row_no == rows - 1, low, 0.0)))
            er, ei = edge
            new_re = partial[0, :, cols] + (DAMPING * er - gains[a] * ei)
            wave[0, :, cols] = new_re
            wave[1, :, cols] = partial[1, :, cols] + (gains[a] * er + DAMPING * ei)
            parts_out[k, :, cols] = new_re

        return carry

    lax.fori_loop(0, steps, step, 0)

    send_part(jnp.int32(steps - 1))
    send_sum(jnp.int32(steps - 1))
    send_sum(jnp.int32(steps - 2))

    for j in range(per):
        k = me * per + j
        near_copy(k).wait_recv()
        across_copy(k).wait_recv()
        image[j] = parts_out[k] + near_in[me // 2, j] + across_in[j]

        @pl.when(k >= steps - DIRECT)
        def _():
            diagonal_copy(k).wait_recv()
            image[j] = image[j] + diagonal_in[k - (steps - DIRECT)]

    for delta in range(1, sections):
        ref_copy(delta).wait_send()

    def drain(k, carry):
        @pl.when(k // per == me)
        def _():
            region_copy(k, across(me), 0).wait_send()
            region_copy(k, partner(me), 1).wait_send()

            @pl.when(k < DIRECT)
            def _():
                region_copy(k, partner(across(me)), 2).wait_send()

        @pl.when(is_across(k))
        def _():
            across_copy(k).wait_send()

            @pl.when(k >= DIRECT)
            def _():
                region_copy(k, partner(me), 1).wait_send()

        @pl.when(is_near(k) | is_diagonal(k))
        def _():
            near_copy(k).wait_send()

        @pl.when(strip < strips - 1)
        def _():
            halo_copy(k, 0).wait_send()

        @pl.when(strip > 0)
        def _():
            halo_copy(k, 1).wait_send()

        return carry

    lax.fori_loop(0, steps, drain, 0)


def shards(sections, strips, surface, omegas, region_speed, fd_coeff, region_index, ref_region):
    freq_count, rows, line_len = surface.shape[1:]
    per = region_index.shape[0]
    steps = per * sections
    chunks = line_len // LANES
    assert freq_count == sections == 4 and chunks == RADIX and per > DIRECT
    weights, twiddle, kx = tables(line_len)
    f32 = jnp.float32
    vmem = pl.BlockSpec(memory_space=pltpu.VMEM)
    dma = pltpu.SemaphoreType.DMA
    return pl.pallas_call(
        functools.partial(kernel, sections, strips),
        out_shape=jax.ShapeDtypeStruct((per, rows, line_len), f32),
        in_specs=[pl.BlockSpec(memory_space=pltpu.HBM)] * 9,
        out_specs=vmem,
        scratch_shapes=[
            pltpu.SMEM(omegas.shape, f32),
            pltpu.SMEM(region_speed.shape, f32),
            pltpu.SMEM(fd_coeff.shape, f32),
            pltpu.SMEM(ref_region.shape, jnp.int32),
            pltpu.VMEM(weights.shape, f32),
            pltpu.VMEM((6 * LANES, 2 * LANES), jnp.bfloat16),
            pltpu.VMEM(twiddle.shape, f32),
            pltpu.VMEM(kx.shape, f32),
            pltpu.VMEM((2, rows, line_len), f32),
            pltpu.VMEM((steps, rows, line_len), jnp.int32),
            pltpu.VMEM((steps, rows, LANES), f32),
            pltpu.VMEM((per, rows, LANES), f32),
            pltpu.VMEM((2, steps, 2 * chunks, LANES), f32),
            pltpu.VMEM((2, steps, 2 * chunks, LANES), f32),
            pltpu.VMEM((steps, rows, line_len), f32),
            pltpu.VMEM((sections // 2, per, rows, line_len), f32),
            pltpu.VMEM((per, rows, line_len), f32),
            pltpu.VMEM((per, rows, line_len), f32),
            pltpu.VMEM((DIRECT, rows, line_len), f32),
            pltpu.VMEM((2, chunks, LANES), f32),
            pltpu.VMEM((2, rows, line_len), f32),
            pltpu.VMEM((2, rows, line_len), f32),
            pltpu.VMEM((rows, LANES), f32),
            pltpu.VMEM((2, rows, line_len), f32),
            dma((9,)),
            dma((sections,)),
            dma((sections,)),
            dma((3, steps)),
            dma((steps,)),
            dma((2, steps)),
            dma((2, steps)),
            dma((steps,)),
            dma((sections // 2, per)),
            dma((per,)),
            dma((per,)),
            dma((DIRECT,)),
        ],
        compiler_params=pltpu.CompilerParams(
            collective_id=0, has_side_effects=True, vmem_limit_bytes=60 * 1024 * 1024
        ),
    )(
        surface, omegas, region_speed, fd_coeff, region_index, ref_region,
        jnp.asarray(weights), jnp.asarray(twiddle), jnp.asarray(kx),
    )


def solution(mesh):
    in_specs = (
        P(None, "shots", "strip", None),
        P(),
        P(),
        P(),
        P("depth", "strip", None),
        P("depth"),
    )
    out_specs = P("depth", "strip", "shots")
    run = functools.partial(shards, mesh.shape["depth"], mesh.shape["strip"])
    return jax.shard_map(run, mesh=mesh, in_specs=in_specs, out_specs=out_specs, check_vma=False)
```

```python
import functools
import math

import jax
import jax.numpy as jnp
import ml_dtypes
import numpy as np
from jax import lax
from jax.experimental import pallas as pl
from jax.experimental.pallas import tpu as pltpu
from jax.sharding import PartitionSpec as P

DAMPING = 0.05
LANES = 128
RADIX = 16
LEAD = 3
SQUARE_MAX = 9.5
MESH = pl.DeviceIdType.MESH


def fitted(function, terms):
    nodes = 0.5 * SQUARE_MAX * (1.0 - np.cos((np.arange(64) + 0.5) * np.pi / 64))
    fit = np.polynomial.Chebyshev.fit(nodes, function(np.sqrt(nodes)), terms - 1, domain=[0, SQUARE_MAX])
    return [float(c) for c in fit.convert(kind=np.polynomial.Polynomial).coef]


COS_TERMS = fitted(np.cos, 9)
SINC_TERMS = fitted(lambda x: np.sin(x) / x, 9)


def horner(terms, square):
    value = jnp.full(square.shape, terms[-1], jnp.float32)
    for term in reversed(terms[:-1]):
        value = value * square + term
    return value


def tables(line_len):
    inner = np.arange(LANES)
    outer = np.arange(RADIX)
    angle = 2.0 * np.pi * (inner[:, None] * inner[None, :] % LANES) / LANES
    cosine, sine = np.cos(angle), np.sin(angle)
    matrix = np.block([[cosine, -sine], [sine, cosine]])
    high = matrix.astype(ml_dtypes.bfloat16)
    low = (matrix - high.astype(np.float64)).astype(ml_dtypes.bfloat16)
    weights = np.concatenate([high, low]).astype(np.float32)
    twist = 2.0 * np.pi * (outer[:, None] * inner[None, :]) / line_len
    twiddle = np.stack([np.cos(twist), np.sin(twist)]).astype(np.float32)
    wave = outer[:, None] + RADIX * inner[None, :]
    signed = np.where(wave >= line_len // 2, wave - line_len, wave)
    kx = signed.astype(np.float32) * np.float32(2.0 * math.pi / line_len)
    return weights, twiddle, kx


def add(a, b):
    return a[0] + b[0], a[1] + b[1]


def sub(a, b):
    return a[0] - b[0], a[1] - b[1]


def times(a, c, s):
    return a[0] * c - a[1] * s, a[0] * s + a[1] * c


def dft4(z):
    even, odd = add(z[0], z[2]), add(z[1], z[3])
    p, r = sub(z[0], z[2]), sub(z[1], z[3])
    turned = (r[1], -r[0])
    return [add(even, odd), (p[0] + r[1], p[1] - r[0]), sub(even, odd), (p[0] - r[1], p[1] + r[0])]


def twist16(z, power):
    if power == 0:
        return z
    if power == 4:
        return z[1], -z[0]
    h = math.sqrt(0.5)
    if power == 2:
        return (z[0] + z[1]) * h, (z[1] - z[0]) * h
    if power == 6:
        return (z[1] - z[0]) * h, (z[0] + z[1]) * (-h)
    angle = -2.0 * math.pi * power / 16
    return times(z, math.cos(angle), math.sin(angle))


def dft16(z):
    mid = [[twist16(v, n * k) for k, v in enumerate(dft4([z[4 * m + n] for m in range(4)]))] for n in range(4)]
    out = [None] * 16
    for k in range(4):
        for j, v in enumerate(dft4([mid[n][k] for n in range(4)])):
            out[k + 4 * j] = v
    return out


def dft128(z, weights):
    stacked = jnp.concatenate(
        [jnp.concatenate([v[0] for v in z], 0), jnp.concatenate([v[1] for v in z], 0)], 1
    )
    high = stacked.astype(jnp.bfloat16)
    low = (stacked - high.astype(jnp.float32)).astype(jnp.bfloat16)
    wide = jnp.concatenate([high, low, high], 1)
    out = jnp.dot(wide, weights, preferred_element_type=jnp.float32)
    rows = z[0][0].shape[0]
    return [
        (out[c * rows:(c + 1) * rows, :LANES], out[c * rows:(c + 1) * rows, LANES:])
        for c in range(len(z))
    ]


def kernel(
    sections, strips, surface, omegas_in, speeds_in, coeffs_in, region, refs_in, weights_in, twiddle_in, kx_in,
    image,
    omegas, speeds, coeffs, refs, raw_weights, weights, twiddle, kx,
    wave, regions, ref_slow, ref_send, halo_out, halo_in, edge_out, edge_in, parts_out, parts_in, mult, phase, gain, gain_rows,
    in_sem, ref_ssem, ref_rsem, reg_ssem, reg_rsem, halo_ssem, halo_rsem, edge_ssem, edge_rsem, img_ssem, img_rsem,
):
    me = lax.axis_index("depth")
    strip = lax.axis_index("strip")
    per = region.shape[0]
    steps = per * sections
    rows = region.shape[1]
    line_len = region.shape[2]
    chunks = line_len // LANES
    tile = (rows, LANES)
    region_count = speeds.shape[0]

    loads = [
        pltpu.make_async_copy(source, target, in_sem.at[n])
        for n, (source, target) in enumerate([
            (refs_in, refs), (speeds_in, speeds), (omegas_in, omegas), (coeffs_in, coeffs),
            (region, regions.at[pl.ds(me * per, per)]), (surface.at[:, me], wave.at[0]),
            (twiddle_in, twiddle), (kx_in, kx), (weights_in, raw_weights),
        ])
    ]
    for load in loads:
        load.start()

    barrier = pltpu.get_barrier_semaphore()
    for delta in range(1, sections):
        pl.semaphore_signal(barrier, 1, device_id={"depth": lax.rem(me + delta, sections)}, device_id_type=MESH)

    @pl.when(strip > 0)
    def _():
        pl.semaphore_signal(barrier, 1, device_id={"strip": strip - 1}, device_id_type=MESH)

    @pl.when(strip < strips - 1)
    def _():
        pl.semaphore_signal(barrier, 1, device_id={"strip": strip + 1}, device_id_type=MESH)

    for load in loads[:4]:
        load.wait()
    row_no = lax.broadcasted_iota(jnp.int32, tile, 0)
    lane_no = lax.broadcasted_iota(jnp.int32, tile, 1)
    omega = jnp.zeros(tile, jnp.float32)
    for f in range(sections):
        omega = jnp.where(jnp.full(tile, me, jnp.int32) == f, omegas[f], omega)
    speed_rows = jnp.full(tile, 1.0, jnp.float32)
    coeff_rows = jnp.zeros(tile, jnp.float32)
    for r in range(region_count):
        speed_rows = jnp.where(row_no == r, speeds[r], speed_rows)
        coeff_rows = jnp.where(row_no == r, coeffs[r], coeff_rows)
    inv_rows = 1.0 / speed_rows
    gain_rows[...] = coeff_rows / omega
    for j in range(per):
        chosen = jnp.full(tile, refs[j], jnp.int32)
        speed_here = jnp.full(tile, 1.0, jnp.float32)
        for r in range(region_count):
            speed_here = jnp.where(chosen == r, speeds[r], speed_here)
        ref_send[j] = 1.0 / speed_here
        ref_slow[me * per + j] = 1.0 / speed_here

    @pl.when(strip == 0)
    def _():
        halo_in[0] = jnp.zeros(halo_in.shape[1:], jnp.float32)
        edge_in[0] = jnp.zeros(edge_in.shape[1:], jnp.int32)

    @pl.when(strip == strips - 1)
    def _():
        halo_in[1] = jnp.zeros(halo_in.shape[1:], jnp.float32)
        edge_in[1] = jnp.zeros(edge_in.shape[1:], jnp.int32)

    def ref_copy(delta):
        return pltpu.make_async_remote_copy(
            ref_send, ref_slow.at[pl.ds(me * per, per)], ref_ssem.at[delta], ref_rsem.at[me],
            device_id={"depth": lax.rem(me + delta, sections)}, device_id_type=MESH,
        )

    def region_copy(j, delta):
        return pltpu.make_async_remote_copy(
            regions.at[me * per + j], regions.at[me * per + j], reg_ssem.at[delta, j], reg_rsem.at[me * per + j],
            device_id={"depth": lax.rem(me + delta, sections)}, device_id_type=MESH,
        )

    def halo_copy(k, side):
        return pltpu.make_async_remote_copy(
            halo_out.at[side, k], halo_in.at[side, k], halo_ssem.at[side, k], halo_rsem.at[side, k],
            device_id={"strip": strip + 1 - 2 * side}, device_id_type=MESH,
        )

    def edge_copy(k, side):
        return pltpu.make_async_remote_copy(
            edge_out.at[side, k], edge_in.at[side, k], edge_ssem.at[side, k], edge_rsem.at[side, k],
            device_id={"strip": strip + 1 - 2 * side}, device_id_type=MESH,
        )

    def send_sides(copy, k):
        @pl.when(strip < strips - 1)
        def _():
            copy(k, 0).start()

        @pl.when(strip > 0)
        def _():
            copy(k, 1).start()

    def wait_sides(copy, k):
        @pl.when(strip > 0)
        def _():
            copy(k, 0).wait_recv()

        @pl.when(strip < strips - 1)
        def _():
            copy(k, 1).wait_recv()

    half = rows // 2

    def swap(cells):
        return pltpu.roll(cells, half, 0)

    def pack(cells):
        down, up = [], []
        for a in range(0, chunks, 2):
            down.append(jnp.where(row_no < half, swap(cells[a]), cells[a + 1]))
            up.append(jnp.where(row_no < half, cells[a], swap(cells[a + 1])))
        return down, up

    def unpack(from_above, from_below):
        ghost = []
        for t in range(chunks // 2):
            ghost.append(jnp.where(row_no < half, from_above[t], swap(from_below[t])))
            ghost.append(jnp.where(row_no < half, swap(from_above[t]), from_below[t]))
        return ghost

    def columns(a):
        return slice(a * LANES, (a + 1) * LANES)

    def chunk(ref, *lead, count=chunks):
        return [ref[(*lead, slice(None), columns(a))] for a in range(count)]

    def send_halo(x):
        for part in range(2):
            for side, cells in enumerate(pack(chunk(wave, 0, part))):
                for t, tile_cells in enumerate(cells):
                    halo_out[side, x, part, :, columns(t)] = tile_cells
        send_sides(halo_copy, x)

    def take_halo(x):
        wait_sides(halo_copy, x)
        for part in range(2):
            ghost = unpack(*[chunk(halo_in, side, x, part, count=chunks // 2) for side in range(2)])
            for a in range(chunks):
                wave[1, part, :, columns(a)] = ghost[a]

    def send_edges(k):
        @pl.when(k // per != me)
        def _():
            pltpu.make_async_remote_copy(
                regions.at[k], regions.at[k], reg_ssem.at[0, 0], reg_rsem.at[k],
                device_id={"depth": me}, device_id_type=MESH,
            ).wait_recv()

        for side, cells in enumerate(pack(chunk(regions, k))):
            for t, tile_cells in enumerate(cells):
                edge_out[side, k, :, columns(t)] = tile_cells
        send_sides(edge_copy, k)

    def image_copy(k):
        return pltpu.make_async_remote_copy(
            parts_out.at[k], parts_in.at[me, lax.rem(k, per)], img_ssem.at[k], img_rsem.at[me, lax.rem(k, per)],
            device_id={"depth": k // per}, device_id_type=MESH,
        )

    pl.semaphore_wait(barrier, sections - 1 + jnp.minimum(strip, 1) + jnp.minimum(strips - 1 - strip, 1))

    for delta in range(1, sections):
        ref_copy(delta).start()

    def send_region(k):
        @pl.when(k // per == me)
        def _():
            for delta in range(1, sections):
                region_copy(lax.rem(k, per), delta).start()

    loads[4].wait()
    for k in range(LEAD):
        send_region(jnp.int32(k))
    loads[5].wait()
    send_halo(jnp.int32(0))
    for load in loads[6:]:
        load.wait()
    for block, source in enumerate((0, 0, 1)):
        weights[block * 2 * LANES:(block + 1) * 2 * LANES] = raw_weights[
            source * 2 * LANES:(source + 1) * 2 * LANES
        ].astype(jnp.bfloat16)
    for delta in range(1, sections):
        source = lax.rem(me + delta, sections)
        pltpu.make_async_remote_copy(
            ref_send, ref_slow.at[pl.ds(source * per, per)], ref_ssem.at[delta], ref_rsem.at[source],
            device_id={"depth": source}, device_id_type=MESH,
        ).wait_recv()

    send_edges(jnp.int32(0))
    send_edges(jnp.int32(1))
    inside = ((row_no < half) & (jnp.full(tile, strip, jnp.int32) > 0)) | (
        (row_no >= half) & (jnp.full(tile, strip, jnp.int32) < strips - 1)
    )

    def prepare(k):
        ref = ref_slow[k]
        wave_ref = omega[:1] * ref[:1]
        excess = wave_ref * wave_ref - kx[...] * kx[...]
        root = jnp.sqrt(jnp.abs(excess))
        live = excess >= 0.0
        square = jnp.maximum(excess, 0.0)
        scale = 1.0 / line_len
        mult[0] = jnp.where(live, horner(COS_TERMS, square), jnp.exp(-root)) * scale
        mult[1] = jnp.where(live, root * horner(SINC_TERMS, square), 0.0) * scale
        angle = omega * (inv_rows - ref)
        square = angle * angle
        turn_cos = horner(COS_TERMS, square)
        turn_sin = angle * horner(SINC_TERMS, square)
        gains = gain_rows[...]
        spread = [
            [jnp.broadcast_to(t[r:r + 1], tile) for r in range(region_count)] for t in (turn_cos, turn_sin, gains)
        ]

        def fill(part, cells, spread):
            for a in range(chunks):
                masks = [(cells[a] & bit) != 0 for bit in (1, 2, 4)]
                found = []
                for level in spread:
                    for mask in masks:
                        level = [jnp.where(mask, level[2 * i + 1], level[2 * i]) for i in range(len(level) // 2)]
                    found.append(level[0])
                phase[part, 0, :, columns(a)] = found[0]
                phase[part, 1, :, columns(a)] = found[1]
                gain[part, :, columns(a)] = found[2]

        fill(0, chunk(regions, k), spread)
        wait_sides(edge_copy, k)
        ghost = unpack(*[chunk(edge_in, side, k, count=chunks // 2) for side in range(2)])
        spread = [[jnp.where(inside, t, 0.0) for t in level] for level in spread[:2]] + spread[2:]
        fill(1, ghost, spread)

    prepare(jnp.int32(0))
    take_halo(jnp.int32(0))

    def step(k, carry):
        twist = [(twiddle[0, c:c + 1], -twiddle[1, c:c + 1]) for c in range(chunks)]

        def twisted(z):
            return [z[0]] + [times(z[c], *twist[c]) for c in range(1, chunks)]

        z = [twisted(dft16(list(zip(chunk(wave, part, 0), chunk(wave, part, 1))))) for part in range(2)]
        z = dft128(z[0] + z[1], weights[...])
        z = [times(v, mult[0, c % chunks:c % chunks + 1], mult[1, c % chunks:c % chunks + 1]) for c, v in enumerate(z)]
        z = dft128([(v[1], v[0]) for v in z], weights[...])
        turned = []
        for part in range(2):
            back = dft16(twisted(z[part * chunks:(part + 1) * chunks]))
            turned.append([
                times((u[1], u[0]), pc, ps) for u, pc, ps in zip(back, chunk(phase, part, 0), chunk(phase, part, 1))
            ])

        def row_of(cells, r):
            return jnp.broadcast_to(cells[r:r + 1], tile)

        laps = []
        for part in range(2):
            both = []
            for comp in range(2):
                v = [[turned[n][a][comp] for a in range(chunks)] for n in range(2)]
                right = [pltpu.roll(cells, 1, 1) for cells in v[part]]
                left = [pltpu.roll(cells, LANES - 1, 1) for cells in v[part]]
                sums = []
                for a in range(chunks):
                    here, other = v[part][a], v[1 - part][a]
                    before = jnp.where(lane_no == 0, right[a - 1], right[a])
                    after = jnp.where(lane_no == LANES - 1, left[(a + 1) % chunks], left[a])
                    above = pltpu.roll(here, 1, 0)
                    below = pltpu.roll(here, rows - 1, 0)
                    if part == 0:
                        above = jnp.where(row_no == 0, row_of(other, half - 1), above)
                        below = jnp.where(row_no == rows - 1, row_of(other, half), below)
                    else:
                        above = jnp.where(row_no == half, row_of(other, rows - 1), above)
                        below = jnp.where(row_no == half - 1, row_of(other, 0), below)
                    sums.append(above + below + before + after - 4.0 * here)
                both.append(sums)
            laps.append(both)
        for part in range(2):
            gains = chunk(gain, part)
            for a in range(chunks):
                lr, li = laps[part][0][a], laps[part][1][a]
                new_re = turned[part][a][0] + (DAMPING * lr - gains[a] * li)
                wave[part, 0, :, columns(a)] = new_re
                wave[part, 1, :, columns(a)] = turned[part][a][1] + (gains[a] * lr + DAMPING * li)
                if part == 0:
                    parts_out[k, :, columns(a)] = new_re

        exchange = (lax.rem(k + 1, half) == 0) & (k + 1 < steps)

        @pl.when(exchange)
        def _():
            send_halo((k + 1) // half)

        @pl.when(k + LEAD < steps)
        def _():
            send_region(k + LEAD)

        @pl.when(k // per != me)
        def _():
            image_copy(k).start()

        @pl.when(k + 2 < steps)
        def _():
            send_edges(k + 2)

        @pl.when(k + 1 < steps)
        def _():
            prepare(k + 1)

        @pl.when(exchange)
        def _():
            take_halo((k + 1) // half)

        return carry

    lax.fori_loop(0, steps, step, 0)

    for j in range(per):
        for delta in range(1, sections):
            source = lax.rem(me + delta, sections)
            pltpu.make_async_remote_copy(
                parts_out.at[0], parts_in.at[source, j], img_ssem.at[0], img_rsem.at[source, j],
                device_id={"depth": source}, device_id_type=MESH,
            ).wait_recv()
        total = parts_out[me * per + j]
        for delta in range(1, sections):
            total = total + parts_in[lax.rem(me + delta, sections), j]
        image[j] = total

    for delta in range(1, sections):
        ref_copy(delta).wait_send()
        for j in range(per):
            region_copy(j, delta).wait_send()

    def drain_sides(copy, k):
        @pl.when(strip < strips - 1)
        def _():
            copy(k, 0).wait_send()

        @pl.when(strip > 0)
        def _():
            copy(k, 1).wait_send()

    for x in range(steps // half):
        drain_sides(halo_copy, x)

    def drain(k, carry):
        @pl.when(k // per != me)
        def _():
            image_copy(k).wait_send()

        drain_sides(edge_copy, k)
        return carry

    lax.fori_loop(0, steps, drain, 0)


def shards(sections, strips, surface, omegas, region_speed, fd_coeff, region_index, ref_region):
    freq_count, rows, line_len = surface.shape[1:]
    per = region_index.shape[0]
    steps = per * sections
    chunks = line_len // LANES
    exchanges = steps // (rows // 2)
    assert steps == exchanges * (rows // 2)
    assert freq_count == sections and chunks == RADIX
    weights, twiddle, kx = tables(line_len)
    f32 = jnp.float32
    vmem = pl.BlockSpec(memory_space=pltpu.VMEM)
    dma = pltpu.SemaphoreType.DMA
    return pl.pallas_call(
        functools.partial(kernel, sections, strips),
        out_shape=jax.ShapeDtypeStruct((per, rows, line_len), f32),
        in_specs=[pl.BlockSpec(memory_space=pltpu.HBM)] * 9,
        out_specs=vmem,
        scratch_shapes=[
            pltpu.SMEM(omegas.shape, f32),
            pltpu.SMEM(region_speed.shape, f32),
            pltpu.SMEM(fd_coeff.shape, f32),
            pltpu.SMEM(ref_region.shape, jnp.int32),
            pltpu.VMEM(weights.shape, f32),
            pltpu.VMEM((6 * LANES, 2 * LANES), jnp.bfloat16),
            pltpu.VMEM(twiddle.shape, f32),
            pltpu.VMEM(kx.shape, f32),
            pltpu.VMEM((2, 2, rows, line_len), f32),
            pltpu.VMEM((steps, rows, line_len), jnp.int32),
            pltpu.VMEM((steps, rows, LANES), f32),
            pltpu.VMEM((per, rows, LANES), f32),
            pltpu.VMEM((2, exchanges, 2, rows, line_len // 2), f32),
            pltpu.VMEM((2, exchanges, 2, rows, line_len // 2), f32),
            pltpu.VMEM((2, steps, rows, line_len // 2), jnp.int32),
            pltpu.VMEM((2, steps, rows, line_len // 2), jnp.int32),
            pltpu.VMEM((steps, rows, line_len), f32),
            pltpu.VMEM((sections, per, rows, line_len), f32),
            pltpu.VMEM((2, chunks, LANES), f32),
            pltpu.VMEM((2, 2, rows, line_len), f32),
            pltpu.VMEM((2, rows, line_len), f32),
            pltpu.VMEM((rows, LANES), f32),
            dma((9,)),
            dma((sections,)),
            dma((sections,)),
            dma((sections, per)),
            dma((steps,)),
            dma((2, exchanges)),
            dma((2, exchanges)),
            dma((2, steps)),
            dma((2, steps)),
            dma((steps,)),
            dma((sections, per)),
        ],
        compiler_params=pltpu.CompilerParams(
            collective_id=0, has_side_effects=True, vmem_limit_bytes=60 * 1024 * 1024
        ),
    )(
        surface, omegas, region_speed, fd_coeff, region_index, ref_region,
        jnp.asarray(weights), jnp.asarray(twiddle), jnp.asarray(kx),
    )


def solution(mesh):
    in_specs = (
        P(None, "shots", "strip", None),
        P(),
        P(),
        P(),
        P("depth", "strip", None),
        P("depth"),
    )
    out_specs = P("depth", "strip", "shots")
    run = functools.partial(shards, mesh.shape["depth"], mesh.shape["strip"])
    return jax.shard_map(run, mesh=mesh, in_specs=in_specs, out_specs=out_specs, check_vma=False)
```

```python
import functools
import math

import jax
import jax.numpy as jnp
import ml_dtypes
import numpy as np
from jax import lax
from jax.experimental import pallas as pl
from jax.experimental.pallas import tpu as pltpu
from jax.sharding import PartitionSpec as P

DAMPING = 0.05
LANES = 128
RADIX = 16
LEAD = 3
SQUARE_MAX = 9.5
MESH = pl.DeviceIdType.MESH


def fitted(function, terms):
    nodes = 0.5 * SQUARE_MAX * (1.0 - np.cos((np.arange(64) + 0.5) * np.pi / 64))
    fit = np.polynomial.Chebyshev.fit(nodes, function(np.sqrt(nodes)), terms - 1, domain=[0, SQUARE_MAX])
    return [float(c) for c in fit.convert(kind=np.polynomial.Polynomial).coef]


COS_TERMS = fitted(np.cos, 9)
SINC_TERMS = fitted(lambda x: np.sin(x) / x, 9)


def horner(terms, square):
    value = jnp.full(square.shape, terms[-1], jnp.float32)
    for term in reversed(terms[:-1]):
        value = value * square + term
    return value


def tables(line_len):
    inner = np.arange(LANES)
    outer = np.arange(RADIX)
    angle = 2.0 * np.pi * (inner[:, None] * inner[None, :] % LANES) / LANES
    cosine, sine = np.cos(angle), np.sin(angle)
    matrix = np.block([[cosine, -sine], [sine, cosine]])
    high = matrix.astype(ml_dtypes.bfloat16)
    low = (matrix - high.astype(np.float64)).astype(ml_dtypes.bfloat16)
    weights = np.concatenate([high, low]).astype(np.float32)
    twist = 2.0 * np.pi * (outer[:, None] * inner[None, :]) / line_len
    twiddle = np.stack([np.cos(twist), np.sin(twist)]).astype(np.float32)
    wave = outer[:, None] + RADIX * inner[None, :]
    signed = np.where(wave >= line_len // 2, wave - line_len, wave)
    kx = signed.astype(np.float32) * np.float32(2.0 * math.pi / line_len)
    return weights, twiddle, kx


def add(a, b):
    return a[0] + b[0], a[1] + b[1]


def sub(a, b):
    return a[0] - b[0], a[1] - b[1]


def times(a, c, s):
    return a[0] * c - a[1] * s, a[0] * s + a[1] * c


def dft4(z):
    even, odd = add(z[0], z[2]), add(z[1], z[3])
    p, r = sub(z[0], z[2]), sub(z[1], z[3])
    turned = (r[1], -r[0])
    return [add(even, odd), (p[0] + r[1], p[1] - r[0]), sub(even, odd), (p[0] - r[1], p[1] + r[0])]


def twist16(z, power):
    if power == 0:
        return z
    if power == 4:
        return z[1], -z[0]
    h = math.sqrt(0.5)
    if power == 2:
        return (z[0] + z[1]) * h, (z[1] - z[0]) * h
    if power == 6:
        return (z[1] - z[0]) * h, (z[0] + z[1]) * (-h)
    angle = -2.0 * math.pi * power / 16
    return times(z, math.cos(angle), math.sin(angle))


def dft16(z):
    mid = [[twist16(v, n * k) for k, v in enumerate(dft4([z[4 * m + n] for m in range(4)]))] for n in range(4)]
    out = [None] * 16
    for k in range(4):
        for j, v in enumerate(dft4([mid[n][k] for n in range(4)])):
            out[k + 4 * j] = v
    return out


def dft128(z, weights):
    stacked = jnp.concatenate(
        [jnp.concatenate([v[0] for v in z], 0), jnp.concatenate([v[1] for v in z], 0)], 1
    )
    high = stacked.astype(jnp.bfloat16)
    low = (stacked - high.astype(jnp.float32)).astype(jnp.bfloat16)
    wide = jnp.concatenate([high, low, high], 1)
    out = jnp.dot(wide, weights, preferred_element_type=jnp.float32)
    rows = z[0][0].shape[0]
    return [
        (out[c * rows:(c + 1) * rows, :LANES], out[c * rows:(c + 1) * rows, LANES:])
        for c in range(len(z))
    ]


def kernel(
    sections, strips, surface, omegas_in, speeds_in, coeffs_in, region, refs_in, weights_in, twiddle_in, kx_in,
    image,
    omegas, speeds, coeffs, refs, raw_weights, weights, twiddle, kx,
    wave, regions, ref_slow, ref_send, halo_out, halo_in, edge_out, edge_in, parts_out, parts_in, mult, phase, gain, gain_rows,
    in_sem, ref_ssem, ref_rsem, reg_ssem, reg_rsem, halo_ssem, halo_rsem, edge_ssem, edge_rsem, img_ssem, img_rsem,
):
    me = lax.axis_index("depth")
    strip = lax.axis_index("strip")
    per = region.shape[0]
    steps = per * sections
    rows = region.shape[1]
    line_len = region.shape[2]
    chunks = line_len // LANES
    tile = (rows, LANES)
    region_count = speeds.shape[0]

    loads = [
        pltpu.make_async_copy(source, target, in_sem.at[n])
        for n, (source, target) in enumerate([
            (refs_in, refs), (speeds_in, speeds), (omegas_in, omegas), (coeffs_in, coeffs),
            (region, regions.at[pl.ds(me * per, per)]), (surface.at[:, me], wave.at[0]),
            (twiddle_in, twiddle), (kx_in, kx), (weights_in, raw_weights),
        ])
    ]
    for load in loads:
        load.start()

    barrier = pltpu.get_barrier_semaphore()
    for delta in range(1, sections):
        pl.semaphore_signal(barrier, 1, device_id={"depth": lax.rem(me + delta, sections)}, device_id_type=MESH)

    @pl.when(strip > 0)
    def _():
        pl.semaphore_signal(barrier, 1, device_id={"strip": strip - 1}, device_id_type=MESH)

    @pl.when(strip < strips - 1)
    def _():
        pl.semaphore_signal(barrier, 1, device_id={"strip": strip + 1}, device_id_type=MESH)

    for load in loads[:4]:
        load.wait()
    row_no = lax.broadcasted_iota(jnp.int32, tile, 0)
    lane_no = lax.broadcasted_iota(jnp.int32, tile, 1)
    omega = jnp.zeros(tile, jnp.float32)
    for f in range(sections):
        omega = jnp.where(jnp.full(tile, me, jnp.int32) == f, omegas[f], omega)
    speed_rows = jnp.full(tile, 1.0, jnp.float32)
    coeff_rows = jnp.zeros(tile, jnp.float32)
    for r in range(region_count):
        speed_rows = jnp.where(row_no == r, speeds[r], speed_rows)
        coeff_rows = jnp.where(row_no == r, coeffs[r], coeff_rows)
    inv_rows = 1.0 / speed_rows
    gain_rows[...] = coeff_rows / omega
    for j in range(per):
        chosen = jnp.full(tile, refs[j], jnp.int32)
        speed_here = jnp.full(tile, 1.0, jnp.float32)
        for r in range(region_count):
            speed_here = jnp.where(chosen == r, speeds[r], speed_here)
        ref_send[j] = 1.0 / speed_here
        ref_slow[me * per + j] = 1.0 / speed_here

    @pl.when(strip == 0)
    def _():
        halo_in[0] = jnp.zeros(halo_in.shape[1:], jnp.float32)
        edge_in[0] = jnp.zeros(edge_in.shape[1:], jnp.int32)

    @pl.when(strip == strips - 1)
    def _():
        halo_in[1] = jnp.zeros(halo_in.shape[1:], jnp.float32)
        edge_in[1] = jnp.zeros(edge_in.shape[1:], jnp.int32)

    def ref_copy(delta):
        return pltpu.make_async_remote_copy(
            ref_send, ref_slow.at[pl.ds(me * per, per)], ref_ssem.at[delta], ref_rsem.at[me],
            device_id={"depth": lax.rem(me + delta, sections)}, device_id_type=MESH,
        )

    def region_copy(j, delta):
        return pltpu.make_async_remote_copy(
            regions.at[me * per + j], regions.at[me * per + j], reg_ssem.at[delta, j], reg_rsem.at[me * per + j],
            device_id={"depth": lax.rem(me + delta, sections)}, device_id_type=MESH,
        )

    def halo_copy(k, side):
        return pltpu.make_async_remote_copy(
            halo_out.at[side, k], halo_in.at[side, k], halo_ssem.at[side, k], halo_rsem.at[side, k],
            device_id={"strip": strip + 1 - 2 * side}, device_id_type=MESH,
        )

    def edge_copy(k, side):
        return pltpu.make_async_remote_copy(
            edge_out.at[side, k], edge_in.at[side, k], edge_ssem.at[side, k], edge_rsem.at[side, k],
            device_id={"strip": strip + 1 - 2 * side}, device_id_type=MESH,
        )

    def send_sides(copy, k):
        @pl.when(strip < strips - 1)
        def _():
            copy(k, 0).start()

        @pl.when(strip > 0)
        def _():
            copy(k, 1).start()

    def wait_sides(copy, k):
        @pl.when(strip > 0)
        def _():
            copy(k, 0).wait_recv()

        @pl.when(strip < strips - 1)
        def _():
            copy(k, 1).wait_recv()

    half = rows // 2

    def swap(cells):
        return pltpu.roll(cells, half, 0)

    def pack(cells):
        down, up = [], []
        for a in range(0, chunks, 2):
            down.append(jnp.where(row_no < half, swap(cells[a]), cells[a + 1]))
            up.append(jnp.where(row_no < half, cells[a], swap(cells[a + 1])))
        return down, up

    def unpack(from_above, from_below):
        ghost = []
        for t in range(chunks // 2):
            ghost.append(jnp.where(row_no < half, from_above[t], swap(from_below[t])))
            ghost.append(jnp.where(row_no < half, swap(from_above[t]), from_below[t]))
        return ghost

    def columns(a):
        return slice(a * LANES, (a + 1) * LANES)

    def chunk(ref, *lead, count=chunks):
        return [ref[(*lead, slice(None), columns(a))] for a in range(count)]

    def send_halo(x):
        for part in range(2):
            for side, cells in enumerate(pack(chunk(wave, 0, part))):
                for t, tile_cells in enumerate(cells):
                    halo_out[side, x, part, :, columns(t)] = tile_cells
        send_sides(halo_copy, x)

    def take_halo(x):
        wait_sides(halo_copy, x)
        for part in range(2):
            ghost = unpack(*[chunk(halo_in, side, x, part, count=chunks // 2) for side in range(2)])
            for a in range(chunks):
                wave[1, part, :, columns(a)] = ghost[a]

    def send_edges(k):
        @pl.when(k // per != me)
        def _():
            pltpu.make_async_remote_copy(
                regions.at[k], regions.at[k], reg_ssem.at[0, 0], reg_rsem.at[k],
                device_id={"depth": me}, device_id_type=MESH,
            ).wait_recv()

        for side, cells in enumerate(pack(chunk(regions, k))):
            for t, tile_cells in enumerate(cells):
                edge_out[side, k, :, columns(t)] = tile_cells
        send_sides(edge_copy, k)

    def image_copy(k):
        return pltpu.make_async_remote_copy(
            parts_out.at[k], parts_in.at[me, lax.rem(k, per)], img_ssem.at[k], img_rsem.at[me, lax.rem(k, per)],
            device_id={"depth": k // per}, device_id_type=MESH,
        )

    pl.semaphore_wait(barrier, sections - 1 + jnp.minimum(strip, 1) + jnp.minimum(strips - 1 - strip, 1))

    for delta in range(1, sections):
        ref_copy(delta).start()

    def send_region(k):
        @pl.when(k // per == me)
        def _():
            for delta in range(1, sections):
                region_copy(lax.rem(k, per), delta).start()

    loads[4].wait()
    for k in range(LEAD):
        send_region(jnp.int32(k))
    loads[5].wait()
    send_halo(jnp.int32(0))
    for load in loads[6:]:
        load.wait()
    for block, source in enumerate((0, 0, 1)):
        weights[block * 2 * LANES:(block + 1) * 2 * LANES] = raw_weights[
            source * 2 * LANES:(source + 1) * 2 * LANES
        ].astype(jnp.bfloat16)
    for delta in range(1, sections):
        source = lax.rem(me + delta, sections)
        pltpu.make_async_remote_copy(
            ref_send, ref_slow.at[pl.ds(source * per, per)], ref_ssem.at[delta], ref_rsem.at[source],
            device_id={"depth": source}, device_id_type=MESH,
        ).wait_recv()

    send_edges(jnp.int32(0))
    inside = ((row_no < half) & (jnp.full(tile, strip, jnp.int32) > 0)) | (
        (row_no >= half) & (jnp.full(tile, strip, jnp.int32) < strips - 1)
    )

    def prepare(k):
        ref = ref_slow[k]
        wave_ref = omega[:1] * ref[:1]
        excess = wave_ref * wave_ref - kx[...] * kx[...]
        root = jnp.sqrt(jnp.abs(excess))
        live = excess >= 0.0
        square = jnp.maximum(excess, 0.0)
        scale = 1.0 / line_len
        mult[0] = jnp.where(live, horner(COS_TERMS, square), jnp.exp(-root)) * scale
        mult[1] = jnp.where(live, root * horner(SINC_TERMS, square), 0.0) * scale
        angle = omega * (inv_rows - ref)
        square = angle * angle
        turn_cos = horner(COS_TERMS, square)
        turn_sin = angle * horner(SINC_TERMS, square)
        gains = gain_rows[...]
        spread = [
            [jnp.broadcast_to(t[r:r + 1], tile) for r in range(region_count)] for t in (turn_cos, turn_sin, gains)
        ]

        def fill(part, cells, spread):
            for a in range(chunks):
                masks = [(cells[a] & bit) != 0 for bit in (1, 2, 4)]
                found = []
                for level in spread:
                    for mask in masks:
                        level = [jnp.where(mask, level[2 * i + 1], level[2 * i]) for i in range(len(level) // 2)]
                    found.append(level[0])
                phase[part, 0, :, columns(a)] = found[0]
                phase[part, 1, :, columns(a)] = found[1]
                gain[part, :, columns(a)] = found[2]

        fill(0, chunk(regions, k), spread)
        wait_sides(edge_copy, k)
        ghost = unpack(*[chunk(edge_in, side, k, count=chunks // 2) for side in range(2)])
        spread = [[jnp.where(inside, t, 0.0) for t in level] for level in spread[:2]] + spread[2:]
        fill(1, ghost, spread)

    prepare(jnp.int32(0))
    send_edges(jnp.int32(1))
    take_halo(jnp.int32(0))

    def step(k, carry):
        twist = [(twiddle[0, c:c + 1], -twiddle[1, c:c + 1]) for c in range(chunks)]

        def twisted(z):
            return [z[0]] + [times(z[c], *twist[c]) for c in range(1, chunks)]

        z = [twisted(dft16(list(zip(chunk(wave, part, 0), chunk(wave, part, 1))))) for part in range(2)]
        z = dft128(z[0] + z[1], weights[...])
        z = [times(v, mult[0, c % chunks:c % chunks + 1], mult[1, c % chunks:c % chunks + 1]) for c, v in enumerate(z)]
        z = dft128([(v[1], v[0]) for v in z], weights[...])
        turned = []
        for part in range(2):
            back = dft16(twisted(z[part * chunks:(part + 1) * chunks]))
            turned.append([
                times((u[1], u[0]), pc, ps) for u, pc, ps in zip(back, chunk(phase, part, 0), chunk(phase, part, 1))
            ])

        def row_of(cells, r):
            return jnp.broadcast_to(cells[r:r + 1], tile)

        laps = []
        for part in range(2):
            both = []
            for comp in range(2):
                v = [[turned[n][a][comp] for a in range(chunks)] for n in range(2)]
                right = [pltpu.roll(cells, 1, 1) for cells in v[part]]
                left = [pltpu.roll(cells, LANES - 1, 1) for cells in v[part]]
                sums = []
                for a in range(chunks):
                    here, other = v[part][a], v[1 - part][a]
                    before = jnp.where(lane_no == 0, right[a - 1], right[a])
                    after = jnp.where(lane_no == LANES - 1, left[(a + 1) % chunks], left[a])
                    above = pltpu.roll(here, 1, 0)
                    below = pltpu.roll(here, rows - 1, 0)
                    if part == 0:
                        above = jnp.where(row_no == 0, row_of(other, half - 1), above)
                        below = jnp.where(row_no == rows - 1, row_of(other, half), below)
                    else:
                        above = jnp.where(row_no == half, row_of(other, rows - 1), above)
                        below = jnp.where(row_no == half - 1, row_of(other, 0), below)
                    sums.append(above + below + before + after - 4.0 * here)
                both.append(sums)
            laps.append(both)
        for part in range(2):
            gains = chunk(gain, part)
            for a in range(chunks):
                lr, li = laps[part][0][a], laps[part][1][a]
                new_re = turned[part][a][0] + (DAMPING * lr - gains[a] * li)
                wave[part, 0, :, columns(a)] = new_re
                wave[part, 1, :, columns(a)] = turned[part][a][1] + (gains[a] * lr + DAMPING * li)
                if part == 0:
                    parts_out[k, :, columns(a)] = new_re

        exchange = (lax.rem(k + 1, half) == 0) & (k + 1 < steps)

        @pl.when(exchange)
        def _():
            send_halo((k + 1) // half)

        @pl.when(k + LEAD < steps)
        def _():
            send_region(k + LEAD)

        @pl.when(k // per != me)
        def _():
            image_copy(k).start()

        @pl.when(k + 2 < steps)
        def _():
            send_edges(k + 2)

        @pl.when(k + 1 < steps)
        def _():
            prepare(k + 1)

        @pl.when(exchange)
        def _():
            take_halo((k + 1) // half)

        return carry

    lax.fori_loop(0, steps, step, 0)

    for j in range(per):
        for delta in range(1, sections):
            source = lax.rem(me + delta, sections)
            pltpu.make_async_remote_copy(
                parts_out.at[0], parts_in.at[source, j], img_ssem.at[0], img_rsem.at[source, j],
                device_id={"depth": source}, device_id_type=MESH,
            ).wait_recv()
        total = parts_out[me * per + j]
        for delta in range(1, sections):
            total = total + parts_in[lax.rem(me + delta, sections), j]
        image[j] = total

    for delta in range(1, sections):
        ref_copy(delta).wait_send()
        for j in range(per):
            region_copy(j, delta).wait_send()

    def drain_sides(copy, k):
        @pl.when(strip < strips - 1)
        def _():
            copy(k, 0).wait_send()

        @pl.when(strip > 0)
        def _():
            copy(k, 1).wait_send()

    for x in range(steps // half):
        drain_sides(halo_copy, x)

    def drain(k, carry):
        @pl.when(k // per != me)
        def _():
            image_copy(k).wait_send()

        drain_sides(edge_copy, k)
        return carry

    lax.fori_loop(0, steps, drain, 0)


def shards(sections, strips, surface, omegas, region_speed, fd_coeff, region_index, ref_region):
    freq_count, rows, line_len = surface.shape[1:]
    per = region_index.shape[0]
    steps = per * sections
    chunks = line_len // LANES
    exchanges = steps // (rows // 2)
    assert steps == exchanges * (rows // 2)
    assert freq_count == sections and chunks == RADIX
    weights, twiddle, kx = tables(line_len)
    f32 = jnp.float32
    vmem = pl.BlockSpec(memory_space=pltpu.VMEM)
    dma = pltpu.SemaphoreType.DMA
    return pl.pallas_call(
        functools.partial(kernel, sections, strips),
        out_shape=jax.ShapeDtypeStruct((per, rows, line_len), f32),
        in_specs=[pl.BlockSpec(memory_space=pltpu.HBM)] * 9,
        out_specs=vmem,
        scratch_shapes=[
            pltpu.SMEM(omegas.shape, f32),
            pltpu.SMEM(region_speed.shape, f32),
            pltpu.SMEM(fd_coeff.shape, f32),
            pltpu.SMEM(ref_region.shape, jnp.int32),
            pltpu.VMEM(weights.shape, f32),
            pltpu.VMEM((6 * LANES, 2 * LANES), jnp.bfloat16),
            pltpu.VMEM(twiddle.shape, f32),
            pltpu.VMEM(kx.shape, f32),
            pltpu.VMEM((2, 2, rows, line_len), f32),
            pltpu.VMEM((steps, rows, line_len), jnp.int32),
            pltpu.VMEM((steps, rows, LANES), f32),
            pltpu.VMEM((per, rows, LANES), f32),
            pltpu.VMEM((2, exchanges, 2, rows, line_len // 2), f32),
            pltpu.VMEM((2, exchanges, 2, rows, line_len // 2), f32),
            pltpu.VMEM((2, steps, rows, line_len // 2), jnp.int32),
            pltpu.VMEM((2, steps, rows, line_len // 2), jnp.int32),
            pltpu.VMEM((steps, rows, line_len), f32),
            pltpu.VMEM((sections, per, rows, line_len), f32),
            pltpu.VMEM((2, chunks, LANES), f32),
            pltpu.VMEM((2, 2, rows, line_len), f32),
            pltpu.VMEM((2, rows, line_len), f32),
            pltpu.VMEM((rows, LANES), f32),
            dma((9,)),
            dma((sections,)),
            dma((sections,)),
            dma((sections, per)),
            dma((steps,)),
            dma((2, exchanges)),
            dma((2, exchanges)),
            dma((2, steps)),
            dma((2, steps)),
            dma((steps,)),
            dma((sections, per)),
        ],
        compiler_params=pltpu.CompilerParams(
            collective_id=0, has_side_effects=True, vmem_limit_bytes=60 * 1024 * 1024
        ),
    )(
        surface, omegas, region_speed, fd_coeff, region_index, ref_region,
        jnp.asarray(weights), jnp.asarray(twiddle), jnp.asarray(kx),
    )


def solution(mesh):
    in_specs = (
        P(None, "shots", "strip", None),
        P(),
        P(),
        P(),
        P("depth", "strip", None),
        P("depth"),
    )
    out_specs = P("depth", "strip", "shots")
    run = functools.partial(shards, mesh.shape["depth"], mesh.shape["strip"])
    return jax.shard_map(run, mesh=mesh, in_specs=in_specs, out_specs=out_specs, check_vma=False)
```
